256 devices in a mesh: dp: 32 (over x, z), proto: 8 (over y, core).
Axes of the slice: x: 4, y: 4, z: 8, core: 2. Of those that a mesh axis runs over, the one named last changes fastest.
Arguments:
- teacher_feat: bfloat16 [16384, 256], P('dp'), may hold values from -16 to 16
- student_feat: bfloat16 [16384, 256], P('dp'), may hold values from -16 to 16
- teacher_protos: bfloat16 [65536, 256], P('proto'), may hold values from -16 to 16
- student_protos: bfloat16 [65536, 256], P('proto'), may hold values from -16 to 16
Outputs:
- row_loss: float32 [16384], P('dp')
- feature_grad: bfloat16 [16384, 256], P('dp')
- proto_grad: bfloat16 [65536, 256], P(('proto', 'dp'))
The draws below stay inside these ranges and needn't reach their ends.
All inputs are finite; a program needn't handle non-finite values.
Results may differ from the reference program's by a relative error of at most 0.0069.
Values may be sent and summed in bfloat16 or wider, within the bound.
No kernel may reach another device: no remote copies, remote signals or barrier semaphores. Data moves between devices by JAX's collectives and lax.ppermute only.
A program may use at most 128 MiB of HBM per device.

```python
import math
import jax
import jax.numpy as jnp
from jax import lax

DIM = 256
PROTOS = 65536
ITERS = 3
BATCH = 16384


def shared_centers(key):
    return jax.random.truncated_normal(jax.random.fold_in(key, 900), -4.0, 4.0, (64, DIM))


def proto_signal(key):
    centers = shared_centers(key)
    inner = jax.random.fold_in(key, 910)
    k_ids, k_str = jax.random.split(inner)
    ids = jax.random.randint(k_ids, (PROTOS,), 0, 64)
    strength = jnp.exp(jax.random.uniform(k_str, (PROTOS, 1), minval=jnp.log(0.3), maxval=jnp.log(3.0)))
    return strength * centers[ids]


def feature_signal(key):
    centers = shared_centers(key)
    inner = jax.random.fold_in(key, 920)
    k_ids, k_str = jax.random.split(inner)
    ids = jax.random.randint(k_ids, (BATCH,), 0, 64)
    strength = jnp.exp(jax.random.uniform(k_str, (BATCH, 1), minval=jnp.log(0.3), maxval=jnp.log(3.0)))
    return strength * centers[ids]


def draw_teacher_feat(key, part):
    signal = feature_signal(key)
    key = jax.random.fold_in(key, 1)
    noise = jax.random.truncated_normal(key, -4.0, 4.0, (BATCH, DIM))
    return (signal + noise).astype(jnp.bfloat16)


def draw_student_feat(key, part):
    signal = feature_signal(key)
    key = jax.random.fold_in(key, 2)
    noise = jax.random.truncated_normal(key, -4.0, 4.0, (BATCH, DIM))
    return (signal + noise).astype(jnp.bfloat16)


def draw_teacher_protos(key, part):
    signal = proto_signal(key)
    key = jax.random.fold_in(key, 3)
    noise = jax.random.truncated_normal(key, -4.0, 4.0, (PROTOS, DIM))
    return (signal + noise).astype(jnp.bfloat16)


def draw_student_protos(key, part):
    signal = proto_signal(key)
    key = jax.random.fold_in(key, 4)
    noise = jax.random.truncated_normal(key, -4.0, 4.0, (PROTOS, DIM))
    return (signal + noise).astype(jnp.bfloat16)


def setup_inputs(seed: int = 0) -> dict:
    keys = jax.random.split(jax.random.key(seed), 5)
    teacher_feat = draw_teacher_feat(jax.random.fold_in(keys[4], 71), 0)
    student_feat = draw_student_feat(jax.random.fold_in(keys[4], 71), 0)
    teacher_protos = draw_teacher_protos(jax.random.fold_in(keys[4], 71), 0)
    student_protos = draw_student_protos(jax.random.fold_in(keys[4], 71), 0)
    return dict(teacher_feat=teacher_feat, student_feat=student_feat, teacher_protos=teacher_protos, student_protos=student_protos)


teacher_temp = 0.07
student_temp = 0.1

def unit_rows(x):
    xf = x.astype(jnp.float32)
    return (xf * lax.rsqrt(lax.optimization_barrier(jnp.sum(xf * xf, axis=1, keepdims=True)) + 1e-06)).astype(jnp.bfloat16)

def by_rows(left, right):
    return lax.dot_general(left, right, (((1,), (1,)), ((), ())), preferred_element_type=jnp.float32)

def reference(teacher_feat, student_feat, teacher_protos, student_protos):
    t_unit = unit_rows(teacher_feat)
    s_unit = unit_rows(student_feat)
    t_dirs = unit_rows(teacher_protos)
    s_dirs = unit_rows(student_protos)
    block = math.gcd(BATCH, 1024)
    count = BATCH // block
    t_blocks = t_unit.reshape(count, block, DIM)
    s_blocks = s_unit.reshape(count, block, DIM)

    def expo_of(tb):
        return jnp.exp(by_rows(tb, t_dirs) / teacher_temp)
    row_scale = jnp.ones((count, block), jnp.float32)
    col_scale = jnp.ones((PROTOS,), jnp.float32)
    row_total = jnp.ones((count, block), jnp.float32)
    for step in range(ITERS):

        def col_step(acc, item):
            tb, rb = item
            return (acc + jnp.dot(rb, expo_of(tb), precision=lax.Precision.HIGHEST, preferred_element_type=jnp.float32), None)
        col, _ = lax.scan(col_step, jnp.zeros((PROTOS,), jnp.float32), (t_blocks, row_scale))
        col_scale = 1.0 / (PROTOS * col)

        def row_step(tb):
            return jnp.dot(expo_of(tb), col_scale, precision=lax.Precision.HIGHEST, preferred_element_type=jnp.float32)
        row_total = lax.map(row_step, t_blocks)
        row_scale = 1.0 / (BATCH * row_total)
    factor = PROTOS / (BATCH * student_temp)

    def final(acc, item):
        tb, sb, rt = item
        targets = expo_of(tb) * col_scale[None, :] / rt[:, None]
        logits = by_rows(sb, s_dirs) / student_temp
        expl = jnp.exp(logits)
        totals = lax.optimization_barrier(jnp.sum(expl, axis=1))
        cross = lax.optimization_barrier(jnp.sum(targets * logits, axis=1))
        loss = jnp.log(totals) - cross
        dlog = ((expl / totals[:, None] - targets) * factor).astype(jnp.bfloat16)
        fgrad = jnp.dot(dlog, s_dirs, preferred_element_type=jnp.float32).astype(jnp.bfloat16)
        acc = acc + lax.dot_general(dlog, sb, (((0,), (0,)), ((), ())), preferred_element_type=jnp.float32)
        return (acc, (loss, fgrad))
    pgrad, outs = lax.scan(final, jnp.zeros((PROTOS, DIM), jnp.float32), (t_blocks, s_blocks, row_total))
    loss, fgrad = outs
    return (loss.reshape(BATCH), fgrad.reshape(BATCH, DIM), pgrad.astype(jnp.bfloat16))
```

```python
import functools
import math

import jax
import jax.numpy as jnp
from jax import lax
from jax.experimental import pallas as pl
from jax.experimental.pallas import tpu as pltpu
from jax.sharding import Mesh, PartitionSpec as P

f32 = jnp.float32
bf16 = jnp.bfloat16

NX, NZ, NY, NC = 4, 8, 4, 2
DIM = 256
PROTOS = 65536
BATCH = 16384
ROWS = BATCH // (NX * NZ)
COLS = PROTOS // (NY * NC)
BK = 1024
NB = COLS // BK
T_EXP2 = math.log2(math.e) / 0.07
S_EXP2 = math.log2(math.e) / 0.1
FACTOR = PROTOS / (BATCH * 0.1)
VMEM = 48 * 1024 * 1024

NT = (((1,), (1,)), ((), ()))
NN = (((1,), (0,)), ((), ()))


def dot(a, b, dims):
    return lax.dot_general(a, b, dims, preferred_element_type=f32)


def unit_rows(x):
    xf = x.astype(f32)
    return (xf * lax.rsqrt(jnp.sum(xf * xf, axis=1, keepdims=True) + 1e-06)).astype(bf16)


def split16(v):
    hi = v.astype(bf16).astype(f32)
    row = lax.broadcasted_iota(jnp.int32, (16, v.shape[1]), 0)
    return jnp.where(row == 0, hi, jnp.where(row == 1, v - hi, 0.0)).astype(bf16)


def lane_fold(m):
    acc = m[:, :128]
    for i in range(1, m.shape[1] // 128):
        acc = acc + m[:, i * 128 : (i + 1) * 128]
    return acc


def to_lanes(acc):
    return jnp.sum(acc.T, axis=0, keepdims=True)


def rows4(v):
    return jnp.concatenate([v[:, i * 128 : (i + 1) * 128] for i in range(4)], axis=0)


def lanes512(m):
    return jnp.concatenate([m[i : i + 1] for i in range(4)], axis=1)


def params():
    return pltpu.CompilerParams(vmem_limit_bytes=VMEM)


def call(kernel, grid, in_specs, out_specs, out_shape, scratch, flops, nbytes, name):
    return pl.pallas_call(
        kernel,
        grid=grid,
        in_specs=in_specs,
        out_specs=out_specs,
        out_shape=out_shape,
        scratch_shapes=scratch,
        compiler_params=params(),
        cost_estimate=pl.CostEstimate(flops=flops, bytes_accessed=nbytes, transcendentals=0),
        name=name,
    )


def whole(*shape):
    return pl.BlockSpec(shape, lambda j: (0,) * len(shape))


def teacher_kernel(feat, protos, unit_o, expo_o, cols_o, unit_s, cols_s):
    j = pl.program_id(0)

    @pl.when(j == 0)
    def _():
        u = unit_rows(feat[...])
        unit_s[...] = u
        unit_o[...] = u

    dirs = unit_rows(protos[...])
    expo = jnp.exp2(dot(unit_s[...], dirs, NT) * T_EXP2)
    expo_o[...] = expo.astype(bf16)
    cols_s[pl.ds(j, 1), :] = jnp.sum(expo, axis=0, keepdims=True)

    @pl.when(j == NB - 1)
    def _():
        cols_o[...] = jnp.broadcast_to(cols_s[...].astype(bf16)[None], cols_o.shape)


def teacher(feat, protos):
    return call(
        teacher_kernel,
        (NB,),
        [whole(ROWS, DIM), pl.BlockSpec((BK, DIM), lambda j: (j, 0))],
        [whole(ROWS, DIM), pl.BlockSpec((ROWS, BK), lambda j: (0, j)), whole(NX * NZ, NB, BK)],
        [
            jax.ShapeDtypeStruct((ROWS, DIM), bf16),
            jax.ShapeDtypeStruct((ROWS, COLS), bf16),
            jax.ShapeDtypeStruct((NX * NZ, NB, BK), bf16),
        ],
        [pltpu.VMEM((ROWS, DIM), bf16), pltpu.VMEM((NB, BK), f32)],
        2 * ROWS * COLS * DIM,
        ROWS * COLS * 2 + COLS * DIM * 2,
        "teacher",
    )(feat, protos)


def student_kernel(feat, protos, unit_o, dirs_o, tot_o, mix_o, unit_s, tot_s):
    j = pl.program_id(0)

    @pl.when(j == 0)
    def _():
        u = unit_rows(feat[...])
        unit_s[...] = u
        unit_o[...] = u
        tot_s[...] = jnp.zeros_like(tot_s)
        mix_o[...] = jnp.zeros_like(mix_o)

    dirs = unit_rows(protos[...])
    dirs_o[...] = dirs
    expl = jnp.exp2(dot(unit_s[...], dirs, NT) * S_EXP2)
    tot_s[...] += lane_fold(expl)
    mix_o[...] += dot(expl.astype(bf16), dirs, NN)

    @pl.when(j == NB - 1)
    def _():
        tot_o[...] = rows4(to_lanes(tot_s[...]))


def student(feat, protos):
    return call(
        student_kernel,
        (NB,),
        [whole(ROWS, DIM), pl.BlockSpec((BK, DIM), lambda j: (j, 0))],
        [whole(ROWS, DIM), pl.BlockSpec((BK, DIM), lambda j: (j, 0)), whole(4, 128), whole(ROWS, DIM)],
        [
            jax.ShapeDtypeStruct((ROWS, DIM), bf16),
            jax.ShapeDtypeStruct((COLS, DIM), bf16),
            jax.ShapeDtypeStruct((4, 128), f32),
            jax.ShapeDtypeStruct((ROWS, DIM), f32),
        ],
        [pltpu.VMEM((ROWS, DIM), bf16), pltpu.VMEM((ROWS, 128), f32)],
        4 * ROWS * COLS * DIM,
        COLS * DIM * 4,
        "student",
    )(feat, protos)


def col_scale(got):
    return 1.0 / (PROTOS * jnp.sum(got[...].astype(f32), axis=0))


def row_kernel(expo, got, rows_o, col_s, acc_s):
    j = pl.program_id(0)

    @pl.when(j == 0)
    def _():
        col_s[...] = col_scale(got)
        acc_s[...] = jnp.zeros_like(acc_s)

    acc_s[...] += dot(split16(col_s[pl.ds(j, 1), :]), expo[...], NT)

    @pl.when(j == NB - 1)
    def _():
        part = rows4(jnp.sum(acc_s[...], axis=0, keepdims=True))
        part = jnp.concatenate([part, jnp.zeros((4, 128), f32)], axis=0)
        rows_o[...] = jnp.broadcast_to(part[None], rows_o.shape)


def row_pass(expo, got):
    return call(
        row_kernel,
        (NB,),
        [pl.BlockSpec((ROWS, BK), lambda j: (0, j)), whole(NX * NZ, NB, BK)],
        whole(NY * NC, 8, 128),
        jax.ShapeDtypeStruct((NY * NC, 8, 128), f32),
        [pltpu.VMEM((NB, BK), f32), pltpu.VMEM((16, ROWS), f32)],
        2 * ROWS * COLS * 16,
        ROWS * COLS * 2,
        "row_pass",
    )(expo, got)


def col_kernel(expo, got, cols_o, lhs_s, cols_s):
    j = pl.program_id(0)

    @pl.when(j == 0)
    def _():
        total = lanes512(jnp.sum(got[...], axis=0)[:4])
        lhs_s[...] = split16(1.0 / (BATCH * total))

    part = dot(lhs_s[...], expo[...], NN)
    cols_s[pl.ds(j, 1), :] = jnp.sum(part, axis=0, keepdims=True)

    @pl.when(j == NB - 1)
    def _():
        cols_o[...] = jnp.broadcast_to(cols_s[...].astype(bf16)[None], cols_o.shape)


def col_pass(expo, got):
    return call(
        col_kernel,
        (NB,),
        [pl.BlockSpec((ROWS, BK), lambda j: (0, j)), whole(NY * NC, 8, 128)],
        whole(NX * NZ, NB, BK),
        jax.ShapeDtypeStruct((NX * NZ, NB, BK), bf16),
        [pltpu.VMEM((16, ROWS), bf16), pltpu.VMEM((NB, BK), f32)],
        2 * ROWS * COLS * 16,
        ROWS * COLS * 2,
        "col_pass",
    )(expo, got)


def last_kernel(expo, got, dirs, unit, tot, stat_o, mix_o, col_o, col_s, acc_s):
    j = pl.program_id(0)

    @pl.when(j == 0)
    def _():
        c = col_scale(got)
        col_s[...] = c
        col_o[...] = c
        acc_s[...] = jnp.zeros_like(acc_s)
        mix_o[...] = jnp.zeros_like(mix_o)

    w = expo[...].astype(f32) * col_s[pl.ds(j, 1), :]
    acc_s[...] += lane_fold(w)
    mix_o[...] += dot(w.astype(bf16), dirs[...], NN)

    @pl.when(j == NB - 1)
    def _():
        part = rows4(to_lanes(acc_s[...]))
        cross = rows4(to_lanes(lane_fold(mix_o[...] * unit[...].astype(f32)))) / 0.1
        stat = jnp.concatenate([part, cross, tot[...], jnp.zeros((4, 128), f32)], axis=0)
        stat_o[...] = jnp.broadcast_to(stat[None], stat_o.shape)


def last_pass(expo, got, dirs, unit, tot):
    n = NZ * NY * NC
    return call(
        last_kernel,
        (NB,),
        [
            pl.BlockSpec((ROWS, BK), lambda j: (0, j)),
            whole(NX * NZ, NB, BK),
            pl.BlockSpec((BK, DIM), lambda j: (j, 0)),
            whole(ROWS, DIM),
            whole(4, 128),
        ],
        [whole(n, 16, 128), whole(ROWS, DIM), whole(NB, BK)],
        [
            jax.ShapeDtypeStruct((n, 16, 128), f32),
            jax.ShapeDtypeStruct((ROWS, DIM), f32),
            jax.ShapeDtypeStruct((NB, BK), f32),
        ],
        [pltpu.VMEM((NB, BK), f32), pltpu.VMEM((ROWS, 128), f32)],
        2 * ROWS * COLS * DIM,
        ROWS * COLS * 2 + COLS * DIM * 2,
        "last_pass",
    )(expo, got, dirs, unit, tot)


def grad_kernel(pos, mine, other, stat, t_protos, s_dirs, col, out, dirs_s, col_s, acc_s, rows_s):
    k = pl.program_id(0)

    @pl.when(k == 0)
    def _():
        acc_s[...] = jnp.zeros_like(acc_s)
        for i in range(NX):
            dirs_s[i] = unit_rows(t_protos[i, 0])
            c = jnp.broadcast_to(col[i : i + 1, :], (128, DIM))
            col_s[i] = c.T

    core = pos[1]
    half = ROWS // NC
    rows_s[pl.ds(pl.multiple_of(core * half, half), half), :] = mine[0]
    rows_s[pl.ds(pl.multiple_of((1 - core) * half, half), half), :] = other[0]
    t_rows = rows_s[:, :DIM]
    s_rows = rows_s[:, DIM:]
    total = jnp.sum(stat[0], axis=0)
    t_scale = FACTOR / lanes512(total[0:4])
    s_scale = FACTOR / lanes512(total[8:12])
    for i in range(NX):
        expo = jnp.exp2(dot(dirs_s[i], t_rows, NT) * T_EXP2)
        expl = jnp.exp2(dot(s_dirs[i, 0], s_rows, NT) * S_EXP2)
        c = col_s[i]
        c = jnp.concatenate([c] * (ROWS // 128), axis=1)
        dlog = (expl * s_scale - expo * c * t_scale).astype(bf16)
        acc_s[i] += dot(dlog, s_rows, NN)

    @pl.when(k == NZ - 1)
    def _():
        out[...] = acc_s[...].astype(bf16)


def proto_part(pos, mine, other, stat, t_protos, s_dirs, col):
    half = ROWS // NC
    grid_spec = pltpu.PrefetchScalarGridSpec(
        num_scalar_prefetch=1,
        grid=(NZ,),
        in_specs=[
            pl.BlockSpec((1, half, 2 * DIM), lambda k, p: (p[2 + k], 0, 0)),
            pl.BlockSpec((1, half, 2 * DIM), lambda k, p: (p[2 + k], 0, 0)),
            pl.BlockSpec((1, NY * NC, 16, 128), lambda k, p: (p[2 + NZ + k], 0, 0, 0)),
            pl.BlockSpec((NX, 1, DIM, DIM), lambda k, p: (0, p[0], 0, 0)),
            pl.BlockSpec((NX, 1, DIM, DIM), lambda k, p: (0, p[0], 0, 0)),
            pl.BlockSpec((NX, DIM), lambda k, p: (0, 0)),
        ],
        out_specs=pl.BlockSpec((NX, DIM, DIM), lambda k, p: (0, 0, 0)),
        scratch_shapes=[
            pltpu.VMEM((NX, DIM, DIM), bf16),
            pltpu.VMEM((NX, DIM, 128), f32),
            pltpu.VMEM((NX, DIM, DIM), f32),
            pltpu.VMEM((ROWS, 2 * DIM), bf16),
        ],
    )
    return pl.pallas_call(
        grad_kernel,
        grid_spec=grid_spec,
        out_shape=jax.ShapeDtypeStruct((NX, DIM, DIM), bf16),
        compiler_params=params(),
        cost_estimate=pl.CostEstimate(
            flops=6 * ROWS * COLS * DIM, bytes_accessed=8 << 20, transcendentals=2 * ROWS * COLS
        ),
        name="proto_part",
    )(pos, mine, other, stat, t_protos, s_dirs, col)


def gather(a, axes):
    return lax.all_to_all(a, axes, 0, 0)


def swap_core(a):
    return lax.ppermute(a, "c", [(0, 1), (1, 0)])


def ring(a):
    up = down = a
    blocks = [a]
    for k in range(NZ // 2):
        up = lax.ppermute(up, "z", [(i, (i + 1) % NZ) for i in range(NZ)])
        blocks.append(up)
        if k < NZ // 2 - 1:
            down = lax.ppermute(down, "z", [(i, (i - 1) % NZ) for i in range(NZ)])
            blocks.append(down)
    return blocks


OFFSETS = (0, -1, 1, -2, 2, -3, 3, -4)


def local(teacher_feat, student_feat, teacher_protos, student_protos):
    z = lax.axis_index("z")
    core = lax.axis_index("c")
    half = ROWS // NC

    t_unit, expo, cols = teacher(teacher_feat, teacher_protos)
    s_unit, s_dirs, tot, s_mix = student(student_feat, student_protos)

    both = jnp.concatenate([t_unit, s_unit], axis=1)
    mine = jnp.stack(ring(lax.dynamic_slice_in_dim(both, core * half, half, 0)))
    other = swap_core(mine)

    for _ in range(2):
        rows = row_pass(expo, gather(cols, ("x", "z")))
        cols = col_pass(expo, gather(rows, ("y", "c")))
    stat, t_mix, col = last_pass(expo, gather(cols, ("x", "z")), s_dirs, s_unit, tot)
    stat = gather(stat, ("z", "y", "c")).reshape(NZ, NY * NC, 16, 128)

    order = (z + jnp.array(OFFSETS, jnp.int32)) % NZ
    pos = jnp.concatenate([jnp.stack([z, core]), jnp.arange(NZ, dtype=jnp.int32), order]).astype(jnp.int32)
    col_mine = lax.dynamic_index_in_dim(col.reshape(NX, NZ, DIM), z, 1, keepdims=False)
    part = proto_part(
        pos,
        mine,
        other,
        stat,
        teacher_protos.reshape(NX, NZ, DIM, DIM),
        s_dirs.reshape(NX, NZ, DIM, DIM),
        col_mine,
    )
    proto_grad = jnp.sum(gather(part, "x").astype(f32), axis=0).astype(bf16)

    own = jnp.sum(lax.dynamic_index_in_dim(stat, z, 0, keepdims=False), axis=0)
    row_total = own[0:4].reshape(ROWS)
    cross = own[4:8].reshape(ROWS) / row_total
    totals = own[8:12].reshape(ROWS)
    row_loss = jnp.log(totals) - cross

    terms = (s_mix / totals[:, None] - t_mix / row_total[:, None]) * FACTOR
    keep = lax.dynamic_slice_in_dim(terms, core * half, half, 0)
    give = lax.dynamic_slice_in_dim(terms, (1 - core) * half, half, 0)
    keep = (keep + swap_core(give.astype(bf16)).astype(f32)).astype(bf16)
    parts = gather(jnp.broadcast_to(keep[None], (NY, half, DIM)), "y")
    done = jnp.sum(parts.astype(f32), axis=0).astype(bf16)
    there = swap_core(done)
    feature_grad = jnp.where(
        core == 0, jnp.concatenate([done, there], 0), jnp.concatenate([there, done], 0)
    )
    return row_loss, feature_grad, proto_grad


def solution(mesh):
    fine = Mesh(mesh.devices.reshape(NX, NZ, NY, NC), ("x", "z", "y", "c"))
    rows, protos = P(("x", "z"), None), P(("y", "c"), None)
    return jax.shard_map(
        local,
        mesh=fine,
        in_specs=(rows, rows, protos, protos),
        out_specs=(P(("x", "z")), rows, P(("y", "c", "x", "z"), None)),
        check_vma=False,
    )
```

```python
import math

import jax
import jax.numpy as jnp
from jax import lax
from jax.experimental import pallas as pl
from jax.experimental.pallas import tpu as pltpu
from jax.sharding import Mesh, PartitionSpec as P

f32 = jnp.float32
bf16 = jnp.bfloat16

NX, NZ, NY, NC = 4, 8, 4, 2
DIM = 256
PROTOS = 65536
BATCH = 16384
ROWS = BATCH // (NX * NZ)
COLS = PROTOS // (NY * NC)
BK = 1024
NB = COLS // BK
T_EXP2 = math.log2(math.e) / 0.07
S_EXP2 = math.log2(math.e) / 0.1
FACTOR = PROTOS / (BATCH * 0.1)
VMEM = 60 * 1024 * 1024
SMALL = 24 * 1024 * 1024

NT = (((1,), (1,)), ((), ()))
NN = (((1,), (0,)), ((), ()))


def dot(a, b, dims):
    return lax.dot_general(a, b, dims, preferred_element_type=f32)


def unit_rows(x):
    xf = x.astype(f32)
    return (xf * lax.rsqrt(jnp.sum(xf * xf, axis=1, keepdims=True) + 1e-06)).astype(bf16)


def lane_fold(m):
    acc = m[:, :128]
    for i in range(1, m.shape[1] // 128):
        acc = acc + m[:, i * 128 : (i + 1) * 128]
    return acc


def to_lanes(acc):
    return jnp.sum(acc.T, axis=0, keepdims=True)


def rows4(v):
    return jnp.concatenate([v[:, i * 128 : (i + 1) * 128] for i in range(4)], axis=0)


def lanes512(m):
    return jnp.concatenate([m[i : i + 1] for i in range(4)], axis=1)


def call(kernel, ins, outs, out_shape, scratch, flops, nbytes, name, limit=VMEM):
    return pl.pallas_call(
        kernel,
        in_specs=ins,
        out_specs=outs,
        out_shape=out_shape,
        scratch_shapes=scratch,
        compiler_params=pltpu.CompilerParams(vmem_limit_bytes=limit),
        cost_estimate=pl.CostEstimate(flops=flops, bytes_accessed=nbytes, transcendentals=0),
        name=name,
    )


ANY = pl.BlockSpec(memory_space=pl.ANY)
INSIDE = pl.BlockSpec(memory_space=pltpu.VMEM)
SCALARS = pl.BlockSpec(memory_space=pltpu.SMEM)
DMA = pltpu.SemaphoreType.DMA


def begin(src, dst, sem):
    copy = pltpu.make_async_copy(src, dst, sem)
    copy.start()
    return copy


def begin_blocks(src, dst, sems):
    for j in range(NB):
        begin(src.at[j], dst.at[j], sems.at[j])


def shape(s, t):
    return jax.ShapeDtypeStruct(s, t)


def teacher_kernel(feat, protos, expo_o, cols_o, feat_s, protos_s, expo_s, logit_s, cols_s, sem, in_sems, out_sems):
    first = begin(feat, feat_s, sem)
    begin_blocks(protos, protos_s, in_sems)
    first.wait()
    feat_s[...] = unit_rows(feat_s[...])

    @pl.loop(0, NB)
    def _(j):
        pltpu.make_async_copy(protos.at[j], protos_s.at[j], in_sems.at[j]).wait()
        sums = []
        for n in range(BK // DIM):
            logit_s[n] = dot(feat_s[...], unit_rows(protos_s[j, n * DIM : (n + 1) * DIM, :]), NT)
            acc = jnp.zeros((8, DIM), f32)
            for r in range(0, ROWS, 64):
                e = jnp.exp2(logit_s[n, r : r + 64, :] * T_EXP2)
                expo_s[j, r : r + 64, n * DIM : (n + 1) * DIM] = e.astype(bf16)
                for q in range(0, 64, 8):
                    acc = acc + e[q : q + 8]
            sums.append(jnp.sum(acc, axis=0, keepdims=True))
        cols_s[pl.ds(j, 1), :] = jnp.concatenate(sums, axis=1)
        pltpu.make_async_copy(expo_s.at[j], expo_o.at[j], out_sems.at[j]).start()

    cols_o[...] = jnp.broadcast_to(cols_s[...].astype(bf16)[None], cols_o.shape)
    for j in range(NB):
        pltpu.make_async_copy(expo_s.at[j], expo_o.at[j], out_sems.at[j]).wait()


def teacher(feat, protos):
    return call(
        teacher_kernel,
        [ANY, ANY],
        [ANY, INSIDE],
        [shape((NB, ROWS, BK), bf16), shape((NX * NZ, NB, BK), bf16)],
        [
            pltpu.VMEM((ROWS, DIM), bf16),
            pltpu.VMEM((NB, BK, DIM), bf16),
            pltpu.VMEM((NB, ROWS, BK), bf16),
            pltpu.VMEM((BK // DIM, ROWS, DIM), f32),
            pltpu.VMEM((NB, BK), f32),
            DMA,
            DMA((NB,)),
            DMA((NB,)),
        ],
        2 * ROWS * COLS * DIM,
        ROWS * COLS * 2 + COLS * DIM * 2,
        "teacher",
    )(feat, protos.reshape(NB, BK, DIM))


def student_kernel(
    feat, protos, dirs_o, tot_o, mix_o, feat_s, protos_s, dirs_s, logit_s, exp_s, tot_s, sem, in_sems, out_sems
):
    first = begin(feat, feat_s, sem)
    begin_blocks(protos, protos_s, in_sems)
    first.wait()
    feat_s[...] = unit_rows(feat_s[...])
    tot_s[...] = jnp.zeros_like(tot_s)
    mix_o[...] = jnp.zeros_like(mix_o)

    @pl.loop(0, NB)
    def _(j):
        pltpu.make_async_copy(protos.at[j], protos_s.at[j], in_sems.at[j]).wait()
        for n in range(BK // DIM):
            part = slice(n * DIM, (n + 1) * DIM)
            dirs = unit_rows(protos_s[j, part, :])
            dirs_s[j, part, :] = dirs
            logit_s[n] = dot(feat_s[...], dirs, NT)
            for r in range(0, ROWS, 64):
                e = jnp.exp2(logit_s[n, r : r + 64, :] * S_EXP2)
                exp_s[r : r + 64, part] = e.astype(bf16)
                tot_s[r : r + 64, :] += lane_fold(e)
        mix_o[...] += dot(exp_s[...], dirs_s[j], NN)
        pltpu.make_async_copy(dirs_s.at[j], dirs_o.at[j], out_sems.at[j]).start()

    tot_o[...] = rows4(to_lanes(tot_s[...]))
    for j in range(NB):
        pltpu.make_async_copy(dirs_s.at[j], dirs_o.at[j], out_sems.at[j]).wait()


def student(feat, protos):
    return call(
        student_kernel,
        [ANY, ANY],
        [ANY, INSIDE, INSIDE],
        [shape((NB, BK, DIM), bf16), shape((4, 128), f32), shape((ROWS, DIM), f32)],
        [
            pltpu.VMEM((ROWS, DIM), bf16),
            pltpu.VMEM((NB, BK, DIM), bf16),
            pltpu.VMEM((NB, BK, DIM), bf16),
            pltpu.VMEM((BK // DIM, ROWS, DIM), f32),
            pltpu.VMEM((ROWS, BK), bf16),
            pltpu.VMEM((ROWS, 128), f32),
            DMA,
            DMA((NB,)),
            DMA((NB,)),
        ],
        4 * ROWS * COLS * DIM,
        COLS * DIM * 4,
        "student",
    )(feat, protos.reshape(NB, BK, DIM))


def col_scale(got):
    return 1.0 / (PROTOS * jnp.sum(got[...].astype(f32), axis=0))


def scaled_rows(expo, col, acc_s, j):
    c = col[pl.ds(j, 1), :]
    cs = [c[:, g * 128 : (g + 1) * 128] for g in range(BK // 128)]
    for r in range(0, ROWS, 32):
        acc = acc_s[r : r + 32, :]
        for g in range(BK // 128):
            acc = acc + expo[j, r : r + 32, g * 128 : (g + 1) * 128].astype(f32) * cs[g]
        acc_s[r : r + 32, :] = acc


def row_last_kernel(expo, got, rows_o, col_o, expo_s, got_s, acc_s, sem, sems):
    first = begin(got, got_s, sem)
    begin_blocks(expo, expo_s, sems)
    acc_s[...] = jnp.zeros_like(acc_s)
    first.wait()
    col_o[...] = col_scale(got_s)

    @pl.loop(0, NB)
    def _(j):
        pltpu.make_async_copy(expo.at[j], expo_s.at[j], sems.at[j]).wait()
        scaled_rows(expo_s, col_o, acc_s, j)

    rows_o[...] = jnp.broadcast_to(rows4(to_lanes(acc_s[...]))[None], rows_o.shape)


def row_last(expo, got):
    return call(
        row_last_kernel,
        [ANY, ANY],
        [INSIDE, INSIDE],
        [shape((NZ * NY * NC, 4, 128), f32), shape((NB, BK), f32)],
        [
            pltpu.VMEM((NB, ROWS, BK), bf16),
            pltpu.VMEM(got.shape, bf16),
            pltpu.VMEM((ROWS, 128), f32),
            DMA,
            DMA((NB,)),
        ],
        2 * ROWS * COLS,
        ROWS * COLS * 2,
        "row_last",
    )(expo, got)


def row_kernel(expo, got, tot, rows_o, got_s, col_s, acc_s, sem):
    first = begin(got, got_s, sem)
    acc_s[...] = jnp.zeros_like(acc_s)
    first.wait()
    col_s[...] = col_scale(got_s[:, :, :BK])

    @pl.loop(0, NB)
    def _(j):
        scaled_rows(expo, col_s, acc_s, j)

    part = jnp.concatenate([rows4(to_lanes(acc_s[...])), tot[...]], axis=0)
    rows_o[...] = jnp.broadcast_to(part[None], rows_o.shape)


def row_pass(held, got, tot):
    return call(
        row_kernel,
        [INSIDE, ANY, INSIDE],
        INSIDE,
        shape((NY * NC, 8, 128), f32),
        [pltpu.VMEM(got.shape, bf16), pltpu.VMEM((NB, BK), f32), pltpu.VMEM((ROWS, 128), f32), DMA],
        2 * ROWS * COLS,
        1 << 16,
        "row_pass",
        SMALL,
    )(pltpu.with_memory_space_constraint(held, pltpu.VMEM), got, tot)


def col_kernel(expo, got, cols_o, tot_o, scale_s, cols_s):
    total = jnp.sum(got[...], axis=0)
    scale_s[...] = jnp.broadcast_to(1.0 / (BATCH * lanes512(total[:4])), (128, ROWS)).T

    @pl.loop(0, NB)
    def _(j):
        accs = [jnp.zeros((8, 128), f32)] * (BK // 128)
        for r in range(0, ROWS, 32):
            scale = scale_s[r : r + 32, :]
            for g in range(BK // 128):
                t = expo[j, r : r + 32, g * 128 : (g + 1) * 128].astype(f32) * scale
                accs[g] = accs[g] + ((t[0:8] + t[8:16]) + (t[16:24] + t[24:32]))
        cols_s[pl.ds(j, 1), :] = jnp.concatenate(
            [jnp.sum(a, axis=0, keepdims=True) for a in accs], axis=1
        )

    cols_o[...] = jnp.broadcast_to(cols_s[...].astype(bf16)[None], cols_o.shape)
    hi = total[4:].astype(bf16).astype(f32)
    tot_o[...] = jnp.concatenate([hi, total[4:] - hi], axis=0).astype(bf16)


def col_pass(held, got, copies):
    return call(
        col_kernel,
        [INSIDE, INSIDE],
        [INSIDE, INSIDE],
        [shape((copies, NB, BK), bf16), shape((8, 128), bf16)],
        [pltpu.VMEM((ROWS, 128), f32), pltpu.VMEM((NB, BK), f32)],
        2 * ROWS * COLS,
        1 << 20,
        "col_pass",
        SMALL,
    )(pltpu.with_memory_space_constraint(held, pltpu.VMEM), got)


def mix_kernel(expo, col, dirs, feat, mix_o, cross_o, expo_s, dirs_s, feat_s, w_s, sem, sems):
    for j in range(NB):
        begin(expo.at[j], expo_s.at[j], sems.at[0, j])
        begin(dirs.at[j], dirs_s.at[j], sems.at[1, j])
    first = begin(feat, feat_s, sem)
    mix_o[...] = jnp.zeros_like(mix_o)

    @pl.loop(0, NB)
    def _(j):
        pltpu.make_async_copy(expo.at[j], expo_s.at[j], sems.at[0, j]).wait()
        c = col[pl.ds(j, 1), :]
        cs = [c[:, g * 128 : (g + 1) * 128] for g in range(BK // 128)]
        for r in range(0, ROWS, 32):
            for g in range(BK // 128):
                part = slice(g * 128, (g + 1) * 128)
                w_s[r : r + 32, part] = (expo_s[j, r : r + 32, part].astype(f32) * cs[g]).astype(bf16)
        pltpu.make_async_copy(dirs.at[j], dirs_s.at[j], sems.at[1, j]).wait()
        mix_o[...] += dot(w_s[...], dirs_s[j], NN)

    first.wait()
    unit = unit_rows(feat_s[...]).astype(f32)
    cross_o[...] = to_lanes(lane_fold(mix_o[...] * unit)) / 0.1


def mix_pass(expo, col, dirs, feat):
    return call(
        mix_kernel,
        [ANY, INSIDE, ANY, ANY],
        [INSIDE, INSIDE],
        [shape((ROWS, DIM), f32), shape((1, ROWS), f32)],
        [
            pltpu.VMEM((NB, ROWS, BK), bf16),
            pltpu.VMEM((NB, BK, DIM), bf16),
            pltpu.VMEM((ROWS, DIM), bf16),
            pltpu.VMEM((ROWS, BK), bf16),
            DMA,
            DMA((2, NB)),
        ],
        2 * ROWS * COLS * DIM,
        ROWS * COLS * 2 + COLS * DIM * 2,
        "mix_pass",
    )(expo, col, dirs, feat)


def early_kernel(*refs):
    pos, mine, other = refs[0], refs[1 : 1 + NZ], refs[1 + NZ : 1 + 2 * NZ]
    (t_protos, s_dirs, got, rows_o, dirs_o, grad_o,
     raw_s, rows_s, t_s, s_s, got_s, d_s, small, sems, outs) = refs[1 + 2 * NZ :]
    z, core = pos[0], pos[1]
    for k in range(NZ):
        begin(mine[k], raw_s.at[k, core], sems.at[0, k])
        begin(other[k], raw_s.at[k, 1 - core], sems.at[1, k])
        if k == 0:
            first = [begin(t_protos.at[i, z], t_s.at[pl.ds(i * DIM, DIM)], small.at[i]) for i in range(NX)]
            first += [begin(s_dirs.at[i, z], s_s.at[pl.ds(i * DIM, DIM)], small.at[NX + i]) for i in range(NX)]
            first.append(begin(got, got_s, small.at[2 * NX]))
    grad_o[...] = jnp.zeros_like(grad_o)
    for copy in first:
        copy.wait()
    dirs_o[...] = unit_rows(t_s[...])

    @pl.loop(0, NZ)
    def _(k):
        pltpu.make_async_copy(mine[0], raw_s.at[k, core], sems.at[0, k]).wait()
        pltpu.make_async_copy(other[0], raw_s.at[k, 1 - core], sems.at[1, k]).wait()
        total = got_s[pos[3 + k]].astype(f32)[:, BK:]
        scale = FACTOR / lanes512(total[:4] + total[4:])
        half = ROWS // NC
        for h in range(NC):
            part = slice(h * half, (h + 1) * half)
            rows_s[k, part, :DIM] = unit_rows(raw_s[k, h, :, :DIM])
            rows_s[k, part, DIM:] = unit_rows(raw_s[k, h, :, DIM:])
        pltpu.make_async_copy(rows_s.at[k], rows_o.at[k], outs.at[k]).start()
        s_rows = rows_s[k, :, DIM:]
        d_s[...] = (jnp.exp2(dot(s_s[...], s_rows, NT) * S_EXP2) * scale).astype(bf16)
        grad_o[...] += dot(d_s[...], s_rows, NN)

    for k in range(NZ):
        pltpu.make_async_copy(rows_s.at[k], rows_o.at[k], outs.at[k]).wait()


def early(pos, mine, other, t_protos, s_dirs, got):
    n, half = NX * DIM, ROWS // NC
    return call(
        early_kernel,
        [SCALARS] + [ANY] * (2 * NZ + 3),
        [ANY, INSIDE, INSIDE],
        [shape((NZ, ROWS, 2 * DIM), bf16), shape((n, DIM), bf16), shape((n, DIM), f32)],
        [
            pltpu.VMEM((NZ, NC, half, 2 * DIM), bf16),
            pltpu.VMEM((NZ, ROWS, 2 * DIM), bf16),
            pltpu.VMEM((n, DIM), bf16),
            pltpu.VMEM((n, DIM), bf16),
            pltpu.VMEM(got.shape, bf16),
            pltpu.VMEM((n, ROWS), bf16),
            DMA((2 * NX + 1,)),
            DMA((2, NZ)),
            DMA((NZ,)),
        ],
        4 * ROWS * COLS * DIM,
        ROWS * COLS,
        "early",
    )(pos, *mine, *other, t_protos, s_dirs, got)


def down_rows(v):
    return jnp.broadcast_to(v, (128, v.shape[1])).T


def scale_rows(m, scale):
    return jnp.concatenate([m[:, g : g + 128] * scale for g in range(0, m.shape[1], 128)], axis=1)


def grad_kernel(
    pos, dirs, rows, stat, got, student_part, col, s_mix, t_mix, cross,
    own_o, next_o, keep_o, give_o, line_o,
    rows_s, stat_s, got_s, dirs_s, part_s, acc_s, s_mix_s, t_mix_s, small, sems,
):
    z, core, x = pos[0], pos[1], pos[2]
    first = [begin(stat, stat_s, small.at[0]), begin(dirs, dirs_s, small.at[1])]
    for k in range(NZ):
        begin(rows.at[k], rows_s.at[k], sems.at[k])
    second = [
        begin(got.at[pl.ds(z, 1)], got_s, small.at[2]),
        begin(s_mix, s_mix_s, small.at[3]),
        begin(t_mix, t_mix_s, small.at[4]),
        begin(student_part, part_s, small.at[5]),
    ]
    acc_s[...] = jnp.zeros_like(acc_s)
    for copy in first:
        copy.wait()

    @pl.loop(0, NZ)
    def _(k):
        total = jnp.sum(stat_s[pos[3 + k]], axis=0)
        scale = down_rows(FACTOR / lanes512(total))
        pltpu.make_async_copy(rows.at[k], rows_s.at[k], sems.at[k]).wait()
        expo = jnp.exp2(dot(dirs_s[...], rows_s[k, :, :DIM], NT) * T_EXP2).astype(bf16)
        r = scale_rows(rows_s[k, :, DIM:].astype(f32), scale).astype(bf16)
        acc_s[...] += dot(expo, r, NN)

    for copy in second:
        copy.wait()
    for d in range(NX):
        i = lax.rem(x + d, NX)
        c = col[pl.ds(2 * i + z // 4, 1), :]
        c = sum(jnp.where(lax.rem(z, 4) == q, c[:, q * DIM : (q + 1) * DIM], 0.0) for q in range(4))
        part = pl.ds(pl.multiple_of(i * DIM, DIM), DIM)
        block = part_s[part, :] - scale_rows(acc_s[part, :], down_rows(c))
        if d == 0:
            own_o[...] = block
        else:
            next_o[d - 1] = block.astype(bf16)

    row_total = lanes512(jnp.sum(stat_s[z], axis=0))
    total = got_s[0].astype(f32)[:, BK:]
    total = lanes512(total[:4] + total[4:])
    s_mix_s[...] = scale_rows(s_mix_s[...], down_rows(FACTOR / total)) - scale_rows(
        t_mix_s[...], down_rows(FACTOR / row_total)
    )
    half = ROWS // NC
    keep_o[:half, :] = s_mix_s[pl.ds(pl.multiple_of(core * half, half), half), :]
    give_o[:half, :] = s_mix_s[pl.ds(pl.multiple_of((1 - core) * half, half), half), :].astype(bf16)
    loss = cross[...] / row_total
    low, high = loss[:, :half], loss[:, half:]
    away = jnp.where(core == 0, high, low)
    hi = away.astype(bf16).astype(f32)
    zeros = jnp.zeros((14, DIM), f32)
    give_o[half:, :] = jnp.concatenate([hi, away - hi, zeros], axis=0).astype(bf16)
    keep_o[half:, :] = jnp.concatenate([jnp.where(core == 0, low, high), zeros[:7]], axis=0)
    line_o[...] = jnp.log(total)


def proto_part(pos, dirs, rows, stat, got, student_part, col, s_mix, t_mix, cross):
    n, half = NX * DIM, ROWS // NC
    return call(
        grad_kernel,
        [SCALARS, ANY, ANY, ANY, ANY, ANY, INSIDE, ANY, ANY, INSIDE],
        [INSIDE] * 5,
        [
            shape((DIM, DIM), f32),
            shape((NX - 1, DIM, DIM), bf16),
            shape((half + 8, DIM), f32),
            shape((half + 16, DIM), bf16),
            shape((1, ROWS), f32),
        ],
        [
            pltpu.VMEM((NZ, ROWS, 2 * DIM), bf16),
            pltpu.VMEM((NZ, NY * NC, 4, 128), f32),
            pltpu.VMEM((1,) + got.shape[1:], bf16),
            pltpu.VMEM((n, DIM), bf16),
            pltpu.VMEM((n, DIM), f32),
            pltpu.VMEM((n, DIM), f32),
            pltpu.VMEM((ROWS, DIM), f32),
            pltpu.VMEM((ROWS, DIM), f32),
            DMA((6,)),
            DMA((NZ,)),
        ],
        4 * ROWS * COLS * DIM,
        ROWS * COLS,
        "proto_part",
    )(pos, dirs, rows, stat, got, student_part, col, s_mix, t_mix, cross)


def gather(a, axes):
    return lax.all_to_all(a, axes, 0, 0)


def swap_core(a):
    return lax.ppermute(a, "c", [(0, 1), (1, 0)])


def shift(a, axis, by):
    n = lax.axis_size(axis)
    return lax.ppermute(a, axis, [(i, (i + by) % n) for i in range(n)])


OFFSETS = (0, -1, 1, -2, 2, -3, 3, -4)


def packed(terms, loss):
    hi = lax.reduce_precision(loss, 8, 7)
    tail = jnp.concatenate([hi, loss - hi, jnp.zeros((14, DIM), f32)], axis=0)
    return jnp.concatenate([terms, tail], axis=0).astype(bf16)


def unpacked(a):
    a = a.astype(f32)
    n = a.shape[0] - 16
    return a[:n], a[n : n + 1] + a[n + 1 : n + 2]


def around(a, axis):
    one, two, three = [shift(a, axis, d).astype(f32) for d in (1, 2, 3)]
    return (a.astype(f32) + two) + (one + three)


def local(teacher_feat, student_feat, teacher_protos, student_protos):
    z = lax.axis_index("z")
    core = lax.axis_index("c")
    half = ROWS // NC
    together = lax.optimization_barrier

    def my_half(a):
        return lax.dynamic_slice_in_dim(a, core * half, half, 0)

    order = (z + jnp.array(OFFSETS, jnp.int32)) % NZ
    pos = jnp.concatenate([jnp.stack([z, core, lax.axis_index("x")]), order]).astype(jnp.int32)

    b0 = jnp.concatenate([my_half(teacher_feat), my_half(student_feat)], axis=1)
    u1, d1 = shift(b0, "z", 1), shift(b0, "z", -1)
    expo, cols = teacher(teacher_feat, teacher_protos)
    cols, u1, d1 = together((cols, u1, d1))

    u2, d2 = shift(u1, "z", 1), shift(d1, "z", -1)
    o0 = swap_core(b0)
    got = gather(cols, ("x", "z"))
    s_dirs, tot, s_mix = student(student_feat, student_protos)
    got, u2, d2, o0, tot = together((got, u2, d2, o0, tot))

    u3, d3 = shift(u2, "z", 1), shift(d2, "z", -1)
    ou1, od1, ou2, od2 = [swap_core(a) for a in (u1, d1, u2, d2)]
    rows = row_pass(expo, got, tot)
    got = gather(rows, ("y", "c"))
    got, u3, d3, ou1, od1, ou2, od2 = together((got, u3, d3, ou1, od1, ou2, od2))

    cols, tots = col_pass(expo, got, 1)
    cols = around(cols[0], "x").astype(bf16)
    cols = jnp.concatenate([cols, tots], axis=1)
    got2 = gather(jnp.broadcast_to(cols[None], (NZ,) + cols.shape), "z")

    u4 = shift(u3, "z", 1)
    ou3, od3 = swap_core(u3), swap_core(d3)
    rows = row_pass(expo, got2, tot)
    got = gather(rows, ("y", "c"))
    got, u4, ou3, od3 = together((got, u4, ou3, od3))

    ou4 = swap_core(u4)
    cols, _ = col_pass(expo, got, NX * NZ)
    cols, ou4 = together((cols, ou4))
    got = gather(cols, ("x", "z"))
    rows_c, dirs_c, student_part = early(
        pos,
        [b0, u1, d1, u2, d2, u3, d3, u4],
        [o0, ou1, od1, ou2, od2, ou3, od3, ou4],
        teacher_protos.reshape(NX, NZ, DIM, DIM),
        s_dirs.reshape(NX, NZ, DIM, DIM),
        got2,
    )
    got, student_part = together((got, student_part))

    rows, col = row_last(expo, got)
    rows, col = together((rows, col))
    stat = gather(rows, ("z", "y", "c")).reshape(NZ, NY * NC, 4, 128)
    t_mix, cross = mix_pass(expo, col, s_dirs, student_feat)
    stat, t_mix, cross = together((stat, t_mix, cross))
    own, following, keep, give, log_total = proto_part(
        pos, dirs_c, rows_c, stat, got2, student_part, col, s_mix, t_mix, cross
    )
    arrived = [shift(following[d], "x", d + 1).astype(f32) for d in range(NX - 1)]
    proto_grad = ((own + arrived[0]) + (arrived[1] + arrived[2])).astype(bf16)

    terms, loss = unpacked(swap_core(give))
    mine = packed(keep[:half] + terms, keep[half : half + 1] + loss)
    terms, loss = unpacked(mine)
    away = [unpacked(shift(mine, "y", d)) for d in (1, 2, 3)]
    terms = (terms + away[1][0]) + (away[0][0] + away[2][0])
    loss = (loss + away[1][1]) + (away[0][1] + away[2][1])
    done = packed(terms, loss)
    there = swap_core(done)
    low, low_loss = unpacked(jnp.where(core == 0, done, there))
    high, high_loss = unpacked(jnp.where(core == 0, there, done))
    feature_grad = jnp.concatenate([low, high], axis=0).astype(bf16)
    row_loss = (log_total - jnp.concatenate([low_loss, high_loss], axis=1)).reshape(ROWS)
    return row_loss, feature_grad, proto_grad


def solution(mesh):
    fine = Mesh(mesh.devices.reshape(NX, NZ, NY, NC), ("x", "z", "y", "c"))
    rows, protos = P(("x", "z"), None), P(("y", "c"), None)
    return jax.shard_map(
        local,
        mesh=fine,
        in_specs=(rows, rows, protos, protos),
        out_specs=(P(("x", "z")), rows, P(("y", "c", "x", "z"), None)),
        check_vma=False,
    )
```

```python
import math

import jax
import jax.numpy as jnp
from jax import lax
from jax.experimental import pallas as pl
from jax.experimental.pallas import tpu as pltpu
from jax.sharding import Mesh, PartitionSpec as P

f32 = jnp.float32
bf16 = jnp.bfloat16

NX, NZ, NY, NC = 4, 8, 4, 2
DIM = 256
PROTOS = 65536
BATCH = 16384
ROWS = BATCH // (NX * NZ)
COLS = PROTOS // (NY * NC)
BK = 1024
NB = COLS // BK
T_EXP2 = math.log2(math.e) / 0.07
S_EXP2 = math.log2(math.e) / 0.1
FACTOR = PROTOS / (BATCH * 0.1)
VMEM = 60 * 1024 * 1024
SMALL = 24 * 1024 * 1024

NT = (((1,), (1,)), ((), ()))
NN = (((1,), (0,)), ((), ()))


def dot(a, b, dims):
    return lax.dot_general(a, b, dims, preferred_element_type=f32)


def unit_rows(x):
    xf = x.astype(f32)
    return (xf * lax.rsqrt(jnp.sum(xf * xf, axis=1, keepdims=True) + 1e-06)).astype(bf16)


def lane_fold(m):
    acc = m[:, :128]
    for i in range(1, m.shape[1] // 128):
        acc = acc + m[:, i * 128 : (i + 1) * 128]
    return acc


def to_lanes(acc):
    return jnp.sum(acc.T, axis=0, keepdims=True)


def rows4(v):
    return jnp.concatenate([v[:, i * 128 : (i + 1) * 128] for i in range(4)], axis=0)


def lanes512(m):
    return jnp.concatenate([m[i : i + 1] for i in range(4)], axis=1)


def call(kernel, ins, outs, out_shape, scratch, flops, nbytes, name, limit=VMEM):
    return pl.pallas_call(
        kernel,
        in_specs=ins,
        out_specs=outs,
        out_shape=out_shape,
        scratch_shapes=scratch,
        compiler_params=pltpu.CompilerParams(vmem_limit_bytes=limit),
        cost_estimate=pl.CostEstimate(flops=flops, bytes_accessed=nbytes, transcendentals=0),
        name=name,
    )


ANY = pl.BlockSpec(memory_space=pl.ANY)
INSIDE = pl.BlockSpec(memory_space=pltpu.VMEM)
SCALARS = pl.BlockSpec(memory_space=pltpu.SMEM)
DMA = pltpu.SemaphoreType.DMA


def begin(src, dst, sem):
    copy = pltpu.make_async_copy(src, dst, sem)
    copy.start()
    return copy


def begin_blocks(src, dst, sems):
    for j in range(NB):
        begin(src.at[j], dst.at[j], sems.at[j])


def shape(s, t):
    return jax.ShapeDtypeStruct(s, t)


def teacher_kernel(feat, protos, expo_o, cols_o, feat_s, protos_s, expo_s, logit_s, cols_s, sem, in_sems, out_sems):
    first = begin(feat, feat_s, sem)
    begin_blocks(protos, protos_s, in_sems)
    first.wait()
    feat_s[...] = unit_rows(feat_s[...])

    @pl.loop(0, NB)
    def _(j):
        pltpu.make_async_copy(protos.at[j], protos_s.at[j], in_sems.at[j]).wait()
        sums = []
        for n in range(BK // DIM):
            logit_s[n] = dot(feat_s[...], unit_rows(protos_s[j, n * DIM : (n + 1) * DIM, :]), NT)
            acc = jnp.zeros((8, DIM), f32)
            for r in range(0, ROWS, 64):
                e = jnp.exp2(logit_s[n, r : r + 64, :] * T_EXP2)
                expo_s[j, r : r + 64, n * DIM : (n + 1) * DIM] = e.astype(bf16)
                for q in range(0, 64, 8):
                    acc = acc + e[q : q + 8]
            sums.append(jnp.sum(acc, axis=0, keepdims=True))
        cols_s[pl.ds(j, 1), :] = jnp.concatenate(sums, axis=1)
        pltpu.make_async_copy(expo_s.at[j], expo_o.at[j], out_sems.at[j]).start()

    cols_o[...] = jnp.broadcast_to(cols_s[...].astype(bf16)[None], cols_o.shape)
    for j in range(NB):
        pltpu.make_async_copy(expo_s.at[j], expo_o.at[j], out_sems.at[j]).wait()


def teacher(feat, protos):
    return call(
        teacher_kernel,
        [ANY, ANY],
        [ANY, INSIDE],
        [shape((NB, ROWS, BK), bf16), shape((NX * NZ, NB, BK), bf16)],
        [
            pltpu.VMEM((ROWS, DIM), bf16),
            pltpu.VMEM((NB, BK, DIM), bf16),
            pltpu.VMEM((NB, ROWS, BK), bf16),
            pltpu.VMEM((BK // DIM, ROWS, DIM), f32),
            pltpu.VMEM((NB, BK), f32),
            DMA,
            DMA((NB,)),
            DMA((NB,)),
        ],
        2 * ROWS * COLS * DIM,
        ROWS * COLS * 2 + COLS * DIM * 2,
        "teacher",
    )(feat, protos.reshape(NB, BK, DIM))


def student_kernel(
    feat, protos, dirs_o, tot_o, mix_o, feat_s, protos_s, dirs_s, logit_s, exp_s, tot_s, sem, in_sems, out_sems
):
    first = begin(feat, feat_s, sem)
    begin_blocks(protos, protos_s, in_sems)
    first.wait()
    feat_s[...] = unit_rows(feat_s[...])
    tot_s[...] = jnp.zeros_like(tot_s)
    mix_o[...] = jnp.zeros_like(mix_o)

    @pl.loop(0, NB, unroll=NB)
    def _(j):
        pltpu.make_async_copy(protos.at[j], protos_s.at[j], in_sems.at[j]).wait()
        for n in range(BK // DIM):
            part = slice(n * DIM, (n + 1) * DIM)
            dirs = unit_rows(protos_s[j, part, :])
            dirs_s[j, part, :] = dirs
            logit_s[n] = dot(feat_s[...], dirs, NT)
            for r in range(0, ROWS, 64):
                e = jnp.exp2(logit_s[n, r : r + 64, :] * S_EXP2)
                exp_s[r : r + 64, part] = e.astype(bf16)
                tot_s[r : r + 64, :] += lane_fold(e)
        mix_o[...] += dot(exp_s[...], dirs_s[j], NN)
        pltpu.make_async_copy(dirs_s.at[j], dirs_o.at[j], out_sems.at[j]).start()

    tot_o[...] = rows4(to_lanes(tot_s[...]))
    for j in range(NB):
        pltpu.make_async_copy(dirs_s.at[j], dirs_o.at[j], out_sems.at[j]).wait()


def student(feat, protos):
    return call(
        student_kernel,
        [ANY, ANY],
        [ANY, INSIDE, INSIDE],
        [shape((NB, BK, DIM), bf16), shape((4, 128), f32), shape((ROWS, DIM), f32)],
        [
            pltpu.VMEM((ROWS, DIM), bf16),
            pltpu.VMEM((NB, BK, DIM), bf16),
            pltpu.VMEM((NB, BK, DIM), bf16),
            pltpu.VMEM((BK // DIM, ROWS, DIM), f32),
            pltpu.VMEM((ROWS, BK), bf16),
            pltpu.VMEM((ROWS, 128), f32),
            DMA,
            DMA((NB,)),
            DMA((NB,)),
        ],
        4 * ROWS * COLS * DIM,
        COLS * DIM * 4,
        "student",
    )(feat, protos.reshape(NB, BK, DIM))


def col_scale(got):
    return 1.0 / (PROTOS * jnp.sum(got[...].astype(f32), axis=0))


def scaled_rows(expo, col, acc_s, j):
    c = col[pl.ds(j, 1), :]
    cs = [c[:, g * 128 : (g + 1) * 128] for g in range(BK // 128)]
    for r in range(0, ROWS, 32):
        acc = acc_s[r : r + 32, :]
        for g in range(BK // 128):
            acc = acc + expo[j, r : r + 32, g * 128 : (g + 1) * 128].astype(f32) * cs[g]
        acc_s[r : r + 32, :] = acc


def row_last_kernel(expo, got, rows_o, col_o, expo_s, got_s, acc_s, sem, sems):
    first = begin(got, got_s, sem)
    begin_blocks(expo, expo_s, sems)
    acc_s[...] = jnp.zeros_like(acc_s)
    first.wait()
    col_o[...] = col_scale(got_s)

    @pl.loop(0, NB)
    def _(j):
        pltpu.make_async_copy(expo.at[j], expo_s.at[j], sems.at[j]).wait()
        scaled_rows(expo_s, col_o, acc_s, j)

    rows_o[...] = jnp.broadcast_to(rows4(to_lanes(acc_s[...]))[None], rows_o.shape)


def row_last(expo, got):
    return call(
        row_last_kernel,
        [ANY, ANY],
        [INSIDE, INSIDE],
        [shape((NZ * NY * NC, 4, 128), f32), shape((NB, BK), f32)],
        [
            pltpu.VMEM((NB, ROWS, BK), bf16),
            pltpu.VMEM(got.shape, bf16),
            pltpu.VMEM((ROWS, 128), f32),
            DMA,
            DMA((NB,)),
        ],
        2 * ROWS * COLS,
        ROWS * COLS * 2,
        "row_last",
    )(expo, got)


def row_kernel(expo, got, tot, rows_o, col_s, acc_s):
    acc_s[...] = jnp.zeros_like(acc_s)
    col_s[...] = col_scale(got[:, :, :BK])

    @pl.loop(0, NB)
    def _(j):
        scaled_rows(expo, col_s, acc_s, j)

    part = jnp.concatenate([rows4(to_lanes(acc_s[...])), tot[...]], axis=0)
    rows_o[...] = jnp.broadcast_to(part[None], rows_o.shape)


def row_pass(held, got, tot):
    return call(
        row_kernel,
        [INSIDE, INSIDE, INSIDE],
        INSIDE,
        shape((NY * NC, 8, 128), f32),
        [pltpu.VMEM((NB, BK), f32), pltpu.VMEM((ROWS, 128), f32)],
        2 * ROWS * COLS,
        1 << 16,
        "row_pass",
        SMALL,
    )(pltpu.with_memory_space_constraint(held, pltpu.VMEM), got, tot)


def col_kernel(expo, got, cols_o, tot_o, scale_s, cols_s):
    total = jnp.sum(got[...], axis=0)
    scale_s[...] = jnp.broadcast_to(1.0 / (BATCH * lanes512(total[:4])), (128, ROWS)).T

    @pl.loop(0, NB)
    def _(j):
        accs = [jnp.zeros((8, 128), f32)] * (BK // 128)
        for r in range(0, ROWS, 32):
            scale = scale_s[r : r + 32, :]
            for g in range(BK // 128):
                t = expo[j, r : r + 32, g * 128 : (g + 1) * 128].astype(f32) * scale
                accs[g] = accs[g] + ((t[0:8] + t[8:16]) + (t[16:24] + t[24:32]))
        cols_s[pl.ds(j, 1), :] = jnp.concatenate(
            [jnp.sum(a, axis=0, keepdims=True) for a in accs], axis=1
        )

    cols_o[...] = jnp.broadcast_to(cols_s[...].astype(bf16)[None], cols_o.shape)
    hi = total[4:].astype(bf16).astype(f32)
    tot_o[...] = jnp.concatenate([hi, total[4:] - hi], axis=0).astype(bf16)


def col_pass(held, got, copies):
    return call(
        col_kernel,
        [INSIDE, INSIDE],
        [INSIDE, INSIDE],
        [shape((copies, NB, BK), bf16), shape((8, 128), bf16)],
        [pltpu.VMEM((ROWS, 128), f32), pltpu.VMEM((NB, BK), f32)],
        2 * ROWS * COLS,
        1 << 20,
        "col_pass",
        SMALL,
    )(pltpu.with_memory_space_constraint(held, pltpu.VMEM), got)


def mix_kernel(expo, col, dirs, feat, mix_o, cross_o, expo_s, dirs_s, feat_s, w_s, sem, sems):
    for j in range(NB):
        begin(expo.at[j], expo_s.at[j], sems.at[0, j])
        begin(dirs.at[j], dirs_s.at[j], sems.at[1, j])
    first = begin(feat, feat_s, sem)
    mix_o[...] = jnp.zeros_like(mix_o)

    @pl.loop(0, NB)
    def _(j):
        pltpu.make_async_copy(expo.at[j], expo_s.at[j], sems.at[0, j]).wait()
        c = col[pl.ds(j, 1), :]
        cs = [c[:, g * 128 : (g + 1) * 128] for g in range(BK // 128)]
        for r in range(0, ROWS, 32):
            for g in range(BK // 128):
                part = slice(g * 128, (g + 1) * 128)
                w_s[r : r + 32, part] = (expo_s[j, r : r + 32, part].astype(f32) * cs[g]).astype(bf16)
        pltpu.make_async_copy(dirs.at[j], dirs_s.at[j], sems.at[1, j]).wait()
        mix_o[...] += dot(w_s[...], dirs_s[j], NN)

    first.wait()
    unit = unit_rows(feat_s[...]).astype(f32)
    cross_o[...] = to_lanes(lane_fold(mix_o[...] * unit)) / 0.1


def mix_pass(expo, col, dirs, feat):
    return call(
        mix_kernel,
        [ANY, INSIDE, ANY, ANY],
        [INSIDE, INSIDE],
        [shape((ROWS, DIM), f32), shape((1, ROWS), f32)],
        [
            pltpu.VMEM((NB, ROWS, BK), bf16),
            pltpu.VMEM((NB, BK, DIM), bf16),
            pltpu.VMEM((ROWS, DIM), bf16),
            pltpu.VMEM((ROWS, BK), bf16),
            DMA,
            DMA((2, NB)),
        ],
        2 * ROWS * COLS * DIM,
        ROWS * COLS * 2 + COLS * DIM * 2,
        "mix_pass",
    )(expo, col, dirs, feat)


def early_kernel(*refs):
    pos, mine, other = refs[0], refs[1 : 1 + NZ], refs[1 + NZ : 1 + 2 * NZ]
    (t_protos, s_dirs, got, rows_o, dirs_o, grad_o,
     raw_s, rows_s, t_s, s_s, got_s, d_s, small, sems, outs) = refs[1 + 2 * NZ :]
    z, core = pos[0], pos[1]
    for k in range(NZ):
        begin(mine[k], raw_s.at[k, core], sems.at[0, k])
        begin(other[k], raw_s.at[k, 1 - core], sems.at[1, k])
        if k == 0:
            first = [begin(t_protos.at[i, z], t_s.at[pl.ds(i * DIM, DIM)], small.at[i]) for i in range(NX)]
            first += [begin(s_dirs.at[i, z], s_s.at[pl.ds(i * DIM, DIM)], small.at[NX + i]) for i in range(NX)]
            first.append(begin(got, got_s, small.at[2 * NX]))
    grad_o[...] = jnp.zeros_like(grad_o)
    for copy in first:
        copy.wait()
    dirs_o[...] = unit_rows(t_s[...])

    @pl.loop(0, NZ, unroll=NZ)
    def _(k):
        pltpu.make_async_copy(mine[0], raw_s.at[k, core], sems.at[0, k]).wait()
        pltpu.make_async_copy(other[0], raw_s.at[k, 1 - core], sems.at[1, k]).wait()
        total = got_s[pos[3 + k]].astype(f32)[:, BK:]
        scale = FACTOR / lanes512(total[:4] + total[4:])
        half = ROWS // NC
        for h in range(NC):
            part = slice(h * half, (h + 1) * half)
            rows_s[k, part, :DIM] = unit_rows(raw_s[k, h, :, :DIM])
            rows_s[k, part, DIM:] = unit_rows(raw_s[k, h, :, DIM:])
        pltpu.make_async_copy(rows_s.at[k], rows_o.at[k], outs.at[k]).start()
        s_rows = rows_s[k, :, DIM:]
        d_s[...] = (jnp.exp2(dot(s_s[...], s_rows, NT) * S_EXP2) * scale).astype(bf16)
        grad_o[...] += dot(d_s[...], s_rows, NN)

    for k in range(NZ):
        pltpu.make_async_copy(rows_s.at[k], rows_o.at[k], outs.at[k]).wait()


def early(pos, mine, other, t_protos, s_dirs, got):
    n, half = NX * DIM, ROWS // NC
    return call(
        early_kernel,
        [SCALARS] + [ANY] * (2 * NZ + 3),
        [ANY, INSIDE, INSIDE],
        [shape((NZ, ROWS, 2 * DIM), bf16), shape((n, DIM), bf16), shape((n, DIM), f32)],
        [
            pltpu.VMEM((NZ, NC, half, 2 * DIM), bf16),
            pltpu.VMEM((NZ, ROWS, 2 * DIM), bf16),
            pltpu.VMEM((n, DIM), bf16),
            pltpu.VMEM((n, DIM), bf16),
            pltpu.VMEM(got.shape, bf16),
            pltpu.VMEM((n, ROWS), bf16),
            DMA((2 * NX + 1,)),
            DMA((2, NZ)),
            DMA((NZ,)),
        ],
        4 * ROWS * COLS * DIM,
        ROWS * COLS,
        "early",
    )(pos, *mine, *other, t_protos, s_dirs, got)


def down_rows(v):
    return jnp.broadcast_to(v, (128, v.shape[1])).T


def scale_rows(m, scale):
    return jnp.concatenate([m[:, g : g + 128] * scale for g in range(0, m.shape[1], 128)], axis=1)


def grad_kernel(
    pos, dirs, rows, stat, got, student_part, col, s_mix, t_mix, cross,
    own_o, next1_o, next2_o, next3_o, keep_o, give_o, line_o,
    rows_s, stat_s, got_s, dirs_s, part_s, acc_s, s_mix_s, t_mix_s, small, sems,
):
    z, core, x = pos[0], pos[1], pos[2]
    first = [begin(stat, stat_s, small.at[0]), begin(dirs, dirs_s, small.at[1])]
    for k in range(NZ):
        begin(rows.at[k], rows_s.at[k], sems.at[k])
    second = [
        begin(got.at[pl.ds(z, 1)], got_s, small.at[2]),
        begin(s_mix, s_mix_s, small.at[3]),
        begin(t_mix, t_mix_s, small.at[4]),
        begin(student_part, part_s, small.at[5]),
    ]
    acc_s[...] = jnp.zeros_like(acc_s)
    for copy in first:
        copy.wait()

    @pl.loop(0, NZ, unroll=NZ)
    def _(k):
        total = jnp.sum(stat_s[pos[3 + k]], axis=0)
        scale = down_rows(FACTOR / lanes512(total))
        pltpu.make_async_copy(rows.at[k], rows_s.at[k], sems.at[k]).wait()
        expo = jnp.exp2(dot(dirs_s[...], rows_s[k, :, :DIM], NT) * T_EXP2).astype(bf16)
        r = scale_rows(rows_s[k, :, DIM:].astype(f32), scale).astype(bf16)
        acc_s[...] += dot(expo, r, NN)

    for copy in second:
        copy.wait()
    for d in range(NX):
        i = lax.rem(x + d, NX)
        c = col[pl.ds(2 * i + z // 4, 1), :]
        c = sum(jnp.where(lax.rem(z, 4) == q, c[:, q * DIM : (q + 1) * DIM], 0.0) for q in range(4))
        part = pl.ds(pl.multiple_of(i * DIM, DIM), DIM)
        block = part_s[part, :] - scale_rows(acc_s[part, :], down_rows(c))
        if d == 0:
            own_o[...] = block
        else:
            (next1_o, next2_o, next3_o)[d - 1][...] = block.astype(bf16)

    row_total = lanes512(jnp.sum(stat_s[z], axis=0))
    total = got_s[0].astype(f32)[:, BK:]
    total = lanes512(total[:4] + total[4:])
    s_mix_s[...] = scale_rows(s_mix_s[...], down_rows(FACTOR / total)) - scale_rows(
        t_mix_s[...], down_rows(FACTOR / row_total)
    )
    half = ROWS // NC
    keep_o[:half, :] = s_mix_s[pl.ds(pl.multiple_of(core * half, half), half), :]
    give_o[:half, :] = s_mix_s[pl.ds(pl.multiple_of((1 - core) * half, half), half), :].astype(bf16)
    loss = cross[...] / row_total
    low, high = loss[:, :half], loss[:, half:]
    away = jnp.where(core == 0, high, low)
    hi = away.astype(bf16).astype(f32)
    zeros = jnp.zeros((14, DIM), f32)
    give_o[half:, :] = jnp.concatenate([hi, away - hi, zeros], axis=0).astype(bf16)
    keep_o[half:, :] = jnp.concatenate([jnp.where(core == 0, low, high), zeros[:7]], axis=0)
    line_o[...] = jnp.log(total)


def proto_part(pos, dirs, rows, stat, got, student_part, col, s_mix, t_mix, cross):
    n, half = NX * DIM, ROWS // NC
    return call(
        grad_kernel,
        [SCALARS] + [ANY] * 5 + [INSIDE, ANY, ANY, INSIDE],
        [INSIDE] * 7,
        [
            shape((DIM, DIM), f32),
            shape((DIM, DIM), bf16),
            shape((DIM, DIM), bf16),
            shape((DIM, DIM), bf16),
            shape((half + 8, DIM), f32),
            shape((half + 16, DIM), bf16),
            shape((1, ROWS), f32),
        ],
        [
            pltpu.VMEM((NZ, ROWS, 2 * DIM), bf16),
            pltpu.VMEM((NZ, NY * NC, 4, 128), f32),
            pltpu.VMEM((1,) + got.shape[1:], bf16),
            pltpu.VMEM((n, DIM), bf16),
            pltpu.VMEM((n, DIM), f32),
            pltpu.VMEM((n, DIM), f32),
            pltpu.VMEM((ROWS, DIM), f32),
            pltpu.VMEM((ROWS, DIM), f32),
            DMA((6,)),
            DMA((NZ,)),
        ],
        4 * ROWS * COLS * DIM,
        ROWS * COLS,
        "proto_part",
    )(pos, dirs, rows, stat, got, student_part, col, s_mix, t_mix, cross)


def gather(a, axes):
    return lax.all_to_all(a, axes, 0, 0)


def swap_core(a):
    return lax.ppermute(a, "c", [(0, 1), (1, 0)])


def shift(a, axis, by):
    n = lax.axis_size(axis)
    return lax.ppermute(a, axis, [(i, (i + by) % n) for i in range(n)])


OFFSETS = (0, -1, 1, -2, 2, -3, 3, -4)


def packed(terms, loss):
    hi = lax.reduce_precision(loss, 8, 7)
    tail = jnp.concatenate([hi, loss - hi, jnp.zeros((14, DIM), f32)], axis=0)
    return jnp.concatenate([terms, tail], axis=0).astype(bf16)


def unpacked(a):
    a = a.astype(f32)
    n = a.shape[0] - 16
    return a[:n], a[n : n + 1] + a[n + 1 : n + 2]


def around(a, axis):
    one, two, three = [shift(a, axis, d).astype(f32) for d in (1, 2, 3)]
    return (a.astype(f32) + two) + (one + three)


def local(teacher_feat, student_feat, teacher_protos, student_protos):
    z = lax.axis_index("z")
    core = lax.axis_index("c")
    half = ROWS // NC
    together = lax.optimization_barrier

    def my_half(a):
        return lax.dynamic_slice_in_dim(a, core * half, half, 0)

    order = (z + jnp.array(OFFSETS, jnp.int32)) % NZ
    pos = jnp.concatenate([jnp.stack([z, core, lax.axis_index("x")]), order]).astype(jnp.int32)

    b0 = jnp.concatenate([my_half(teacher_feat), my_half(student_feat)], axis=1)
    u1, d1 = shift(b0, "z", 1), shift(b0, "z", -1)
    expo, cols = teacher(teacher_feat, teacher_protos)
    cols, u1, d1 = together((cols, u1, d1))

    u2, d2 = shift(u1, "z", 1), shift(d1, "z", -1)
    o0, ou1, od1 = swap_core(b0), swap_core(u1), swap_core(d1)
    got = gather(cols, ("x", "z"))
    s_dirs, tot, s_mix = student(student_feat, student_protos)
    got, u2, d2, o0, ou1, od1, tot = together((got, u2, d2, o0, ou1, od1, tot))

    u3, d3 = shift(u2, "z", 1), shift(d2, "z", -1)
    ou2, od2 = swap_core(u2), swap_core(d2)
    rows = row_pass(expo, got, tot)
    rows, u3, d3, ou2, od2 = together((rows, u3, d3, ou2, od2))
    got = gather(rows, ("y", "c"))

    got, u3, d3 = together((got, u3, d3))
    u4, ou3, od3 = shift(u3, "z", 1), swap_core(u3), swap_core(d3)
    cols, tots = col_pass(expo, got, 1)
    cols = around(cols[0], "x").astype(bf16)
    cols = jnp.concatenate([cols, tots], axis=1)
    cols, u4, ou3, od3 = together((cols, u4, ou3, od3))
    got2 = gather(jnp.broadcast_to(cols[None], (NZ,) + cols.shape), "z")

    ou4 = swap_core(u4)
    rows = row_pass(expo, got2, tot)
    rows, ou4 = together((rows, ou4))
    got = gather(rows, ("y", "c"))
    cols, _ = col_pass(expo, got, NX * NZ)

    got = gather(cols, ("x", "z"))
    rows_c, dirs_c, student_part = early(
        pos,
        [b0, u1, d1, u2, d2, u3, d3, u4],
        [o0, ou1, od1, ou2, od2, ou3, od3, ou4],
        teacher_protos.reshape(NX, NZ, DIM, DIM),
        s_dirs.reshape(NX, NZ, DIM, DIM),
        got2,
    )
    got, student_part = together((got, student_part))

    rows, col = row_last(expo, got)
    rows, col = together((rows, col))
    stat = gather(rows, ("z", "y", "c")).reshape(NZ, NY * NC, 4, 128)
    t_mix, cross = mix_pass(expo, col, s_dirs, student_feat)
    stat, t_mix, cross = together((stat, t_mix, cross))
    own, next1, next2, next3, keep, give, log_total = proto_part(
        pos, dirs_c, rows_c, stat, got2, student_part, col, s_mix, t_mix, cross
    )
    arrived = [shift(a, "x", d).astype(f32) for a, d in ((next1, 1), (next2, 2), (next3, 3))]
    proto_grad = ((own + arrived[0]) + (arrived[1] + arrived[2])).astype(bf16)

    terms, loss = unpacked(swap_core(give))
    mine = packed(keep[:half] + terms, keep[half : half + 1] + loss)
    terms, loss = unpacked(mine)
    away = [unpacked(shift(mine, "y", d)) for d in (1, 2, 3)]
    terms = (terms + away[1][0]) + (away[0][0] + away[2][0])
    loss = (loss + away[1][1]) + (away[0][1] + away[2][1])
    done = packed(terms, loss)
    there = swap_core(done)
    low, low_loss = unpacked(jnp.where(core == 0, done, there))
    high, high_loss = unpacked(jnp.where(core == 0, there, done))
    feature_grad = jnp.concatenate([low, high], axis=0).astype(bf16)
    row_loss = (log_total - jnp.concatenate([low_loss, high_loss], axis=1)).reshape(ROWS)
    return row_loss, feature_grad, proto_grad


def solution(mesh):
    fine = Mesh(mesh.devices.reshape(NX, NZ, NY, NC), ("x", "z", "y", "c"))
    rows, protos = P(("x", "z"), None), P(("y", "c"), None)
    return jax.shard_map(
        local,
        mesh=fine,
        in_specs=(rows, rows, protos, protos),
        out_specs=(P(("x", "z")), rows, P(("y", "c", "x", "z"), None)),
        check_vma=False,
    )
```

```python
import math

import jax
import jax.numpy as jnp
from jax import lax
from jax.experimental import pallas as pl
from jax.experimental.pallas import tpu as pltpu
from jax.sharding import Mesh, PartitionSpec as P

f32 = jnp.float32
bf16 = jnp.bfloat16

NX, NZ, NY, NC = 4, 8, 4, 2
DIM = 256
PROTOS = 65536
BATCH = 16384
ROWS = BATCH // (NX * NZ)
COLS = PROTOS // (NY * NC)
BK = 1024
NB = COLS // BK
T_EXP2 = math.log2(math.e) / 0.07
S_EXP2 = math.log2(math.e) / 0.1
FACTOR = PROTOS / (BATCH * 0.1)
VMEM = 60 * 1024 * 1024
SMALL = 24 * 1024 * 1024
MIDDLE = 48 * 1024 * 1024

NT = (((1,), (1,)), ((), ()))
NN = (((1,), (0,)), ((), ()))


def dot(a, b, dims):
    return lax.dot_general(a, b, dims, preferred_element_type=f32)


def unit_rows(x):
    xf = x.astype(f32)
    return (xf * lax.rsqrt(jnp.sum(xf * xf, axis=1, keepdims=True) + 1e-06)).astype(bf16)


def lane_fold(m):
    acc = m[:, :128]
    for i in range(1, m.shape[1] // 128):
        acc = acc + m[:, i * 128 : (i + 1) * 128]
    return acc


def to_lanes(acc):
    return jnp.sum(acc.T, axis=0, keepdims=True)


def rows4(v):
    return jnp.concatenate([v[:, i * 128 : (i + 1) * 128] for i in range(4)], axis=0)


def lanes512(m):
    return jnp.concatenate([m[i : i + 1] for i in range(4)], axis=1)


def call(kernel, ins, outs, out_shape, scratch, flops, nbytes, name, limit=VMEM):
    return pl.pallas_call(
        kernel,
        in_specs=ins,
        out_specs=outs,
        out_shape=out_shape,
        scratch_shapes=scratch,
        compiler_params=pltpu.CompilerParams(vmem_limit_bytes=limit),
        cost_estimate=pl.CostEstimate(flops=flops, bytes_accessed=nbytes, transcendentals=0),
        name=name,
    )


ANY = pl.BlockSpec(memory_space=pl.ANY)
INSIDE = pl.BlockSpec(memory_space=pltpu.VMEM)
SCALARS = pl.BlockSpec(memory_space=pltpu.SMEM)
DMA = pltpu.SemaphoreType.DMA


def begin(src, dst, sem):
    copy = pltpu.make_async_copy(src, dst, sem)
    copy.start()
    return copy


def begin_blocks(src, dst, sems):
    for j in range(NB):
        begin(src.at[j], dst.at[j], sems.at[j])


def shape(s, t):
    return jax.ShapeDtypeStruct(s, t)


def teacher_kernel(feat, protos, expo_o, cols_o, feat_s, protos_s, expo_s, logit_s, cols_s, sem, in_sems, out_sems):
    first = begin(feat, feat_s, sem)
    begin_blocks(protos, protos_s, in_sems)
    first.wait()
    feat_s[...] = unit_rows(feat_s[...])

    @pl.loop(0, NB)
    def _(j):
        pltpu.make_async_copy(protos.at[j], protos_s.at[j], in_sems.at[j]).wait()
        sums = []
        for n in range(BK // DIM):
            logit_s[n] = dot(feat_s[...], unit_rows(protos_s[j, n * DIM : (n + 1) * DIM, :]), NT)
            acc = jnp.zeros((8, DIM), f32)
            for r in range(0, ROWS, 64):
                e = jnp.exp2(logit_s[n, r : r + 64, :] * T_EXP2)
                expo_s[j, r : r + 64, n * DIM : (n + 1) * DIM] = e.astype(bf16)
                for q in range(0, 64, 8):
                    acc = acc + e[q : q + 8]
            sums.append(jnp.sum(acc, axis=0, keepdims=True))
        cols_s[pl.ds(j, 1), :] = jnp.concatenate(sums, axis=1)
        pltpu.make_async_copy(expo_s.at[j], expo_o.at[j], out_sems.at[j]).start()

    cols_o[...] = jnp.broadcast_to(cols_s[...].astype(bf16)[None], cols_o.shape)
    for j in range(NB):
        pltpu.make_async_copy(expo_s.at[j], expo_o.at[j], out_sems.at[j]).wait()


def teacher(feat, protos):
    return call(
        teacher_kernel,
        [ANY, ANY],
        [ANY, INSIDE],
        [shape((NB, ROWS, BK), bf16), shape((NX * NZ, NB, BK), bf16)],
        [
            pltpu.VMEM((ROWS, DIM), bf16),
            pltpu.VMEM((NB, BK, DIM), bf16),
            pltpu.VMEM((NB, ROWS, BK), bf16),
            pltpu.VMEM((BK // DIM, ROWS, DIM), f32),
            pltpu.VMEM((NB, BK), f32),
            DMA,
            DMA((NB,)),
            DMA((NB,)),
        ],
        2 * ROWS * COLS * DIM,
        ROWS * COLS * 2 + COLS * DIM * 2,
        "teacher",
    )(feat, protos.reshape(NB, BK, DIM))


def student_kernel(
    feat, protos, dirs_o, tot_o, mix_o, feat_s, protos_s, dirs_s, logit_s, exp_s, tot_s, sem, in_sems, out_sems
):
    first = begin(feat, feat_s, sem)
    begin_blocks(protos, protos_s, in_sems)
    first.wait()
    feat_s[...] = unit_rows(feat_s[...])
    tot_s[...] = jnp.zeros_like(tot_s)
    mix_o[...] = jnp.zeros_like(mix_o)

    @pl.loop(0, NB, unroll=NB)
    def _(j):
        pltpu.make_async_copy(protos.at[j], protos_s.at[j], in_sems.at[j]).wait()
        for n in range(BK // DIM):
            part = slice(n * DIM, (n + 1) * DIM)
            dirs = unit_rows(protos_s[j, part, :])
            dirs_s[j, part, :] = dirs
            logit_s[n] = dot(feat_s[...], dirs, NT)
            for r in range(0, ROWS, 64):
                e = jnp.exp2(logit_s[n, r : r + 64, :] * S_EXP2)
                exp_s[r : r + 64, part] = e.astype(bf16)
                tot_s[r : r + 64, :] += lane_fold(e)
        mix_o[...] += dot(exp_s[...], dirs_s[j], NN)
        pltpu.make_async_copy(dirs_s.at[j], dirs_o.at[j], out_sems.at[j]).start()

    tot_o[...] = rows4(to_lanes(tot_s[...]))
    for j in range(NB):
        pltpu.make_async_copy(dirs_s.at[j], dirs_o.at[j], out_sems.at[j]).wait()


def student(feat, protos):
    return call(
        student_kernel,
        [ANY, ANY],
        [ANY, INSIDE, INSIDE],
        [shape((NB, BK, DIM), bf16), shape((4, 128), f32), shape((ROWS, DIM), f32)],
        [
            pltpu.VMEM((ROWS, DIM), bf16),
            pltpu.VMEM((NB, BK, DIM), bf16),
            pltpu.VMEM((NB, BK, DIM), bf16),
            pltpu.VMEM((BK // DIM, ROWS, DIM), f32),
            pltpu.VMEM((ROWS, BK), bf16),
            pltpu.VMEM((ROWS, 128), f32),
            DMA,
            DMA((NB,)),
            DMA((NB,)),
        ],
        4 * ROWS * COLS * DIM,
        COLS * DIM * 4,
        "student",
    )(feat, protos.reshape(NB, BK, DIM))


def col_scale(got):
    return 1.0 / (PROTOS * jnp.sum(got[...].astype(f32), axis=0))


def scaled_rows(expo, col, acc_s, j):
    c = col[pl.ds(j, 1), :]
    cs = [c[:, g * 128 : (g + 1) * 128] for g in range(BK // 128)]
    for r in range(0, ROWS, 32):
        acc = acc_s[r : r + 32, :]
        for g in range(BK // 128):
            acc = acc + expo[j, r : r + 32, g * 128 : (g + 1) * 128].astype(f32) * cs[g]
        acc_s[r : r + 32, :] = acc


def row_sums(expo, got, col, acc_s):
    acc_s[...] = jnp.zeros_like(acc_s)
    col[...] = col_scale(got[:, :, :BK])

    @pl.loop(0, NB)
    def _(j):
        scaled_rows(expo, col, acc_s, j)

    return rows4(to_lanes(acc_s[...]))


def row_kernel(expo, got, tot, rows_o, col_s, acc_s, tot_s, sem):
    first = begin(tot, tot_s, sem)
    part = row_sums(expo, got, col_s, acc_s)
    first.wait()
    part = jnp.concatenate([part, tot_s[...]], axis=0)
    rows_o[...] = jnp.broadcast_to(part[None], rows_o.shape)


def row_pass(held, got, tot):
    return call(
        row_kernel,
        [INSIDE, INSIDE, ANY],
        INSIDE,
        shape((NY * NC, 8, 128), f32),
        [pltpu.VMEM((NB, BK), f32), pltpu.VMEM((ROWS, 128), f32), pltpu.VMEM((4, 128), f32), DMA],
        2 * ROWS * COLS,
        1 << 16,
        "row_pass",
        SMALL,
    )(pltpu.with_memory_space_constraint(held, pltpu.VMEM), got, tot)


def row_last_kernel(expo, got, rows_o, col_o, acc_s):
    part = row_sums(expo, got, col_o, acc_s)
    rows_o[...] = jnp.broadcast_to(part[None], rows_o.shape)


def row_last(held, got):
    return call(
        row_last_kernel,
        [INSIDE, INSIDE],
        [INSIDE, INSIDE],
        [shape((NZ * NY * NC, 4, 128), f32), shape((NB, BK), f32)],
        [pltpu.VMEM((ROWS, 128), f32)],
        2 * ROWS * COLS,
        1 << 16,
        "row_last",
        SMALL,
    )(pltpu.with_memory_space_constraint(held, pltpu.VMEM), got)


def col_kernel(expo, got, cols_o, tot_o, scale_s, cols_s):
    total = jnp.sum(got[...], axis=0)
    scale_s[...] = jnp.broadcast_to(1.0 / (BATCH * lanes512(total[:4])), (128, ROWS)).T

    @pl.loop(0, NB)
    def _(j):
        accs = [jnp.zeros((8, 128), f32)] * (BK // 128)
        for r in range(0, ROWS, 32):
            scale = scale_s[r : r + 32, :]
            for g in range(BK // 128):
                t = expo[j, r : r + 32, g * 128 : (g + 1) * 128].astype(f32) * scale
                accs[g] = accs[g] + ((t[0:8] + t[8:16]) + (t[16:24] + t[24:32]))
        cols_s[pl.ds(j, 1), :] = jnp.concatenate(
            [jnp.sum(a, axis=0, keepdims=True) for a in accs], axis=1
        )

    cols_o[...] = jnp.broadcast_to(cols_s[...].astype(bf16)[None], cols_o.shape)
    hi = total[4:].astype(bf16).astype(f32)
    tot_o[...] = jnp.concatenate([hi, total[4:] - hi], axis=0).astype(bf16)


def col_pass(held, got, copies):
    return call(
        col_kernel,
        [INSIDE, INSIDE],
        [INSIDE, INSIDE],
        [shape((copies, NB, BK), bf16), shape((8, 128), bf16)],
        [pltpu.VMEM((ROWS, 128), f32), pltpu.VMEM((NB, BK), f32)],
        2 * ROWS * COLS,
        1 << 20,
        "col_pass",
        SMALL,
    )(pltpu.with_memory_space_constraint(held, pltpu.VMEM), got)


def mix_kernel(expo, col, dirs, feat, mix_o, cross_o, expo_s, dirs_s, feat_s, w_s, sem, sems):
    for j in range(NB):
        begin(expo.at[j], expo_s.at[j], sems.at[0, j])
        begin(dirs.at[j], dirs_s.at[j], sems.at[1, j])
    first = begin(feat, feat_s, sem)
    mix_o[...] = jnp.zeros_like(mix_o)

    @pl.loop(0, NB)
    def _(j):
        pltpu.make_async_copy(expo.at[j], expo_s.at[j], sems.at[0, j]).wait()
        c = col[pl.ds(j, 1), :]
        cs = [c[:, g * 128 : (g + 1) * 128] for g in range(BK // 128)]
        for r in range(0, ROWS, 32):
            for g in range(BK // 128):
                part = slice(g * 128, (g + 1) * 128)
                w_s[r : r + 32, part] = (expo_s[j, r : r + 32, part].astype(f32) * cs[g]).astype(bf16)
        pltpu.make_async_copy(dirs.at[j], dirs_s.at[j], sems.at[1, j]).wait()
        mix_o[...] += dot(w_s[...], dirs_s[j], NN)

    first.wait()
    unit = unit_rows(feat_s[...]).astype(f32)
    cross_o[...] = to_lanes(lane_fold(mix_o[...] * unit)) / 0.1


def mix_pass(expo, col, dirs, feat):
    return call(
        mix_kernel,
        [ANY, INSIDE, ANY, ANY],
        [INSIDE, INSIDE],
        [shape((ROWS, DIM), f32), shape((1, ROWS), f32)],
        [
            pltpu.VMEM((NB, ROWS, BK), bf16),
            pltpu.VMEM((NB, BK, DIM), bf16),
            pltpu.VMEM((ROWS, DIM), bf16),
            pltpu.VMEM((ROWS, BK), bf16),
            DMA,
            DMA((2, NB)),
        ],
        2 * ROWS * COLS * DIM,
        ROWS * COLS * 2 + COLS * DIM * 2,
        "mix_pass",
    )(expo, col, dirs, feat)


def early_kernel(*refs):
    pos, mine, other = refs[0], refs[1 : 1 + NZ], refs[1 + NZ : 1 + 2 * NZ]
    (t_protos, s_dirs, got, rows_o, dirs_o, grad_o,
     raw_s, rows_s, t_s, s_s, got_s, d_s, small, sems, outs) = refs[1 + 2 * NZ :]
    z, core = pos[0], pos[1]
    for k in range(NZ):
        begin(mine[k], raw_s.at[k, core], sems.at[0, k])
        begin(other[k], raw_s.at[k, 1 - core], sems.at[1, k])
        if k == 0:
            first = [begin(t_protos.at[i, z], t_s.at[pl.ds(i * DIM, DIM)], small.at[i]) for i in range(NX)]
            first += [begin(s_dirs.at[i, z], s_s.at[pl.ds(i * DIM, DIM)], small.at[NX + i]) for i in range(NX)]
            first.append(begin(got, got_s, small.at[2 * NX]))
    grad_o[...] = jnp.zeros_like(grad_o)
    for copy in first:
        copy.wait()
    dirs_o[...] = unit_rows(t_s[...])

    @pl.loop(0, NZ, unroll=NZ)
    def _(k):
        pltpu.make_async_copy(mine[0], raw_s.at[k, core], sems.at[0, k]).wait()
        pltpu.make_async_copy(other[0], raw_s.at[k, 1 - core], sems.at[1, k]).wait()
        total = got_s[pos[3 + k]].astype(f32)[:, BK:]
        scale = FACTOR / lanes512(total[:4] + total[4:])
        half = ROWS // NC
        for h in range(NC):
            part = slice(h * half, (h + 1) * half)
            rows_s[k, part, :DIM] = unit_rows(raw_s[k, h, :, :DIM])
            rows_s[k, part, DIM:] = unit_rows(raw_s[k, h, :, DIM:])
        pltpu.make_async_copy(rows_s.at[k], rows_o.at[k], outs.at[k]).start()
        s_rows = rows_s[k, :, DIM:]
        d_s[...] = (jnp.exp2(dot(s_s[...], s_rows, NT) * S_EXP2) * scale).astype(bf16)
        grad_o[...] += dot(d_s[...], s_rows, NN)

    for k in range(NZ):
        pltpu.make_async_copy(rows_s.at[k], rows_o.at[k], outs.at[k]).wait()


def early(pos, mine, other, t_protos, s_dirs, got):
    n, half = NX * DIM, ROWS // NC
    return call(
        early_kernel,
        [SCALARS] + [ANY] * (2 * NZ + 3),
        [ANY, INSIDE, INSIDE],
        [shape((NZ, ROWS, 2 * DIM), bf16), shape((n, DIM), bf16), shape((n, DIM), f32)],
        [
            pltpu.VMEM((NZ, NC, half, 2 * DIM), bf16),
            pltpu.VMEM((NZ, ROWS, 2 * DIM), bf16),
            pltpu.VMEM((n, DIM), bf16),
            pltpu.VMEM((n, DIM), bf16),
            pltpu.VMEM(got.shape, bf16),
            pltpu.VMEM((n, ROWS), bf16),
            DMA((2 * NX + 1,)),
            DMA((2, NZ)),
            DMA((NZ,)),
        ],
        4 * ROWS * COLS * DIM,
        ROWS * COLS,
        "early",
    )(pos, *mine, *other, t_protos, s_dirs, got)


def down_rows(v):
    return jnp.broadcast_to(v, (128, v.shape[1])).T


def scale_rows(m, scale):
    return jnp.concatenate([m[:, g : g + 128] * scale for g in range(0, m.shape[1], 128)], axis=1)


def grad_kernel(
    pos, dirs, rows, stat, got, student_part, col, s_mix, t_mix, cross,
    own_o, next1_o, next2_o, next3_o, keep_o, give_o, line_o,
    rows_s, got_s, dirs_s, part_s, acc_s, s_mix_s, t_mix_s, small, sems,
):
    z, core, x = pos[0], pos[1], pos[2]
    first = [begin(dirs, dirs_s, small.at[1])]
    for k in range(NZ):
        begin(rows.at[k], rows_s.at[k], sems.at[k])
    second = [
        begin(got.at[pl.ds(z, 1)], got_s, small.at[2]),
        begin(s_mix, s_mix_s, small.at[3]),
        begin(t_mix, t_mix_s, small.at[4]),
        begin(student_part, part_s, small.at[5]),
    ]
    acc_s[...] = jnp.zeros_like(acc_s)
    for copy in first:
        copy.wait()

    @pl.loop(0, NZ, unroll=NZ)
    def _(k):
        total = jnp.sum(stat[pos[3 + k]], axis=0)
        scale = down_rows(FACTOR / lanes512(total))
        pltpu.make_async_copy(rows.at[k], rows_s.at[k], sems.at[k]).wait()
        expo = jnp.exp2(dot(dirs_s[...], rows_s[k, :, :DIM], NT) * T_EXP2).astype(bf16)
        r = scale_rows(rows_s[k, :, DIM:].astype(f32), scale).astype(bf16)
        acc_s[...] += dot(expo, r, NN)

    for copy in second:
        copy.wait()
    for d in range(NX):
        i = lax.rem(x + d, NX)
        c = col[pl.ds(2 * i + z // 4, 1), :]
        c = sum(jnp.where(lax.rem(z, 4) == q, c[:, q * DIM : (q + 1) * DIM], 0.0) for q in range(4))
        part = pl.ds(pl.multiple_of(i * DIM, DIM), DIM)
        block = part_s[part, :] - scale_rows(acc_s[part, :], down_rows(c))
        if d == 0:
            own_o[...] = block
        else:
            (next1_o, next2_o, next3_o)[d - 1][...] = block.astype(bf16)

    row_total = lanes512(jnp.sum(stat[z], axis=0))
    total = got_s[0].astype(f32)[:, BK:]
    total = lanes512(total[:4] + total[4:])
    s_mix_s[...] = scale_rows(s_mix_s[...], down_rows(FACTOR / total)) - scale_rows(
        t_mix_s[...], down_rows(FACTOR / row_total)
    )
    half = ROWS // NC
    keep_o[:half, :] = s_mix_s[pl.ds(pl.multiple_of(core * half, half), half), :]
    give_o[:half, :] = s_mix_s[pl.ds(pl.multiple_of((1 - core) * half, half), half), :].astype(bf16)
    loss = cross[...] / row_total
    low, high = loss[:, :half], loss[:, half:]
    away = jnp.where(core == 0, high, low)
    hi = away.astype(bf16).astype(f32)
    zeros = jnp.zeros((14, DIM), f32)
    give_o[half:, :] = jnp.concatenate([hi, away - hi, zeros], axis=0).astype(bf16)
    keep_o[half:, :] = jnp.concatenate([jnp.where(core == 0, low, high), zeros[:7]], axis=0)
    line_o[...] = jnp.log(total)


def proto_part(pos, dirs, rows, stat, got, student_part, col, s_mix, t_mix, cross):
    n, half = NX * DIM, ROWS // NC
    return call(
        grad_kernel,
        [SCALARS, ANY, ANY, INSIDE, ANY, ANY, INSIDE, ANY, ANY, INSIDE],
        [INSIDE] * 7,
        [
            shape((DIM, DIM), f32),
            shape((DIM, DIM), bf16),
            shape((DIM, DIM), bf16),
            shape((DIM, DIM), bf16),
            shape((half + 8, DIM), f32),
            shape((half + 16, DIM), bf16),
            shape((1, ROWS), f32),
        ],
        [
            pltpu.VMEM((NZ, ROWS, 2 * DIM), bf16),
            pltpu.VMEM((1,) + got.shape[1:], bf16),
            pltpu.VMEM((n, DIM), bf16),
            pltpu.VMEM((n, DIM), f32),
            pltpu.VMEM((n, DIM), f32),
            pltpu.VMEM((ROWS, DIM), f32),
            pltpu.VMEM((ROWS, DIM), f32),
            DMA((6,)),
            DMA((NZ,)),
        ],
        4 * ROWS * COLS * DIM,
        ROWS * COLS,
        "proto_part",
        MIDDLE,
    )(pos, dirs, rows, stat, got, student_part, col, s_mix, t_mix, cross)


def gather(a, axes):
    return lax.all_to_all(a, axes, 0, 0)


def swap_core(a):
    return lax.ppermute(a, "c", [(0, 1), (1, 0)])


def shift(a, axis, by):
    n = lax.axis_size(axis)
    return lax.ppermute(a, axis, [(i, (i + by) % n) for i in range(n)])


OFFSETS = (0, -1, 1, -2, 2, -3, 3, -4)


def packed(terms, loss):
    hi = lax.reduce_precision(loss, 8, 7)
    tail = jnp.concatenate([hi, loss - hi, jnp.zeros((14, DIM), f32)], axis=0)
    return jnp.concatenate([terms, tail], axis=0).astype(bf16)


def unpacked(a):
    a = a.astype(f32)
    n = a.shape[0] - 16
    return a[:n], a[n : n + 1] + a[n + 1 : n + 2]


def around(a, axis):
    one, two, three = [shift(a, axis, d).astype(f32) for d in (1, 2, 3)]
    return (a.astype(f32) + two) + (one + three)


def local(teacher_feat, student_feat, teacher_protos, student_protos):
    z = lax.axis_index("z")
    core = lax.axis_index("c")
    half = ROWS // NC
    together = lax.optimization_barrier

    def my_half(a):
        return lax.dynamic_slice_in_dim(a, core * half, half, 0)

    order = (z + jnp.array(OFFSETS, jnp.int32)) % NZ
    pos = jnp.concatenate([jnp.stack([z, core, lax.axis_index("x")]), order]).astype(jnp.int32)

    b0 = jnp.concatenate([my_half(teacher_feat), my_half(student_feat)], axis=1)
    u1, d1 = shift(b0, "z", 1), shift(b0, "z", -1)
    expo, cols = teacher(teacher_feat, teacher_protos)
    cols, u1, d1 = together((cols, u1, d1))

    u2, d2 = shift(u1, "z", 1), shift(d1, "z", -1)
    o0, ou1, od1 = swap_core(b0), swap_core(u1), swap_core(d1)
    got = gather(cols, ("x", "z"))
    s_dirs, tot, s_mix = student(student_feat, student_protos)
    got, u2, d2, o0, ou1, od1, tot = together((got, u2, d2, o0, ou1, od1, tot))

    u3, d3 = shift(u2, "z", 1), shift(d2, "z", -1)
    ou2, od2 = swap_core(u2), swap_core(d2)
    rows = row_pass(expo, got, tot)
    rows, u3, d3, ou2, od2 = together((rows, u3, d3, ou2, od2))
    got = gather(rows, ("y", "c"))

    got, u3, d3 = together((got, u3, d3))
    u4 = shift(u3, "z", 1)
    cols, tots = col_pass(expo, got, 1)
    cols = around(cols[0], "x").astype(bf16)
    cols = jnp.concatenate([cols, tots], axis=1)
    cols, u4 = together((cols, u4))
    got2 = gather(jnp.broadcast_to(cols[None], (NZ,) + cols.shape), "z")

    got2, u3, d3, u4 = together((got2, u3, d3, u4))
    ou3, od3, ou4 = swap_core(u3), swap_core(d3), swap_core(u4)
    rows = row_pass(expo, got2, tot)
    rows, ou3, od3, ou4 = together((rows, ou3, od3, ou4))
    got = gather(rows, ("y", "c"))
    cols, _ = col_pass(expo, got, NX * NZ)

    got = gather(cols, ("x", "z"))
    rows_c, dirs_c, student_part = early(
        pos,
        [b0, u1, d1, u2, d2, u3, d3, u4],
        [o0, ou1, od1, ou2, od2, ou3, od3, ou4],
        teacher_protos.reshape(NX, NZ, DIM, DIM),
        s_dirs.reshape(NX, NZ, DIM, DIM),
        got2,
    )
    got, student_part = together((got, student_part))

    rows, col = row_last(expo, got)
    rows, col = together((rows, col))
    stat = gather(rows, ("z", "y", "c")).reshape(NZ, NY * NC, 4, 128)
    t_mix, cross = mix_pass(expo, col, s_dirs, student_feat)
    stat, t_mix, cross = together((stat, t_mix, cross))
    own, next1, next2, next3, keep, give, log_total = proto_part(
        pos, dirs_c, rows_c, stat, got2, student_part, col, s_mix, t_mix, cross
    )
    arrived = [shift(a, "x", d).astype(f32) for a, d in ((next1, 1), (next2, 2), (next3, 3))]
    proto_grad = ((own + arrived[0]) + (arrived[1] + arrived[2])).astype(bf16)

    terms, loss = unpacked(swap_core(give))
    mine = packed(keep[:half] + terms, keep[half : half + 1] + loss)
    terms, loss = unpacked(mine)
    away = [unpacked(shift(mine, "y", d)) for d in (1, 2, 3)]
    terms = (terms + away[1][0]) + (away[0][0] + away[2][0])
    loss = (loss + away[1][1]) + (away[0][1] + away[2][1])
    done = packed(terms, loss)
    there = swap_core(done)
    low, low_loss = unpacked(jnp.where(core == 0, done, there))
    high, high_loss = unpacked(jnp.where(core == 0, there, done))
    feature_grad = jnp.concatenate([low, high], axis=0).astype(bf16)
    row_loss = (log_total - jnp.concatenate([low_loss, high_loss], axis=1)).reshape(ROWS)
    return row_loss, feature_grad, proto_grad


def solution(mesh):
    fine = Mesh(mesh.devices.reshape(NX, NZ, NY, NC), ("x", "z", "y", "c"))
    rows, protos = P(("x", "z"), None), P(("y", "c"), None)
    return jax.shard_map(
        local,
        mesh=fine,
        in_specs=(rows, rows, protos, protos),
        out_specs=(P(("x", "z")), rows, P(("y", "c", "x", "z"), None)),
        check_vma=False,
    )
```

```python
import math

import jax
import jax.numpy as jnp
from jax import lax
from jax.experimental import pallas as pl
from jax.experimental.pallas import tpu as pltpu
from jax.sharding import Mesh, PartitionSpec as P

f32 = jnp.float32
bf16 = jnp.bfloat16

NX, NZ, NY, NC = 4, 8, 4, 2
DIM = 256
PROTOS = 65536
BATCH = 16384
ROWS = BATCH // (NX * NZ)
COLS = PROTOS // (NY * NC)
BK = 1024
NB = COLS // BK
T_EXP2 = math.log2(math.e) / 0.07
S_EXP2 = math.log2(math.e) / 0.1
FACTOR = PROTOS / (BATCH * 0.1)
VMEM = 60 * 1024 * 1024
SMALL = 24 * 1024 * 1024
MIDDLE = 48 * 1024 * 1024

NT = (((1,), (1,)), ((), ()))
NN = (((1,), (0,)), ((), ()))


def dot(a, b, dims):
    return lax.dot_general(a, b, dims, preferred_element_type=f32)


def unit_rows(x):
    xf = x.astype(f32)
    return (xf * lax.rsqrt(jnp.sum(xf * xf, axis=1, keepdims=True) + 1e-06)).astype(bf16)


def lane_fold(m):
    acc = m[:, :128]
    for i in range(1, m.shape[1] // 128):
        acc = acc + m[:, i * 128 : (i + 1) * 128]
    return acc


def to_lanes(acc):
    return jnp.sum(acc.T, axis=0, keepdims=True)


def rows4(v):
    return jnp.concatenate([v[:, i * 128 : (i + 1) * 128] for i in range(4)], axis=0)


def lanes512(m):
    return jnp.concatenate([m[i : i + 1] for i in range(4)], axis=1)


def call(kernel, ins, outs, out_shape, scratch, flops, nbytes, name, limit=VMEM):
    return pl.pallas_call(
        kernel,
        in_specs=ins,
        out_specs=outs,
        out_shape=out_shape,
        scratch_shapes=scratch,
        compiler_params=pltpu.CompilerParams(vmem_limit_bytes=limit),
        cost_estimate=pl.CostEstimate(flops=flops, bytes_accessed=nbytes, transcendentals=0),
        name=name,
    )


ANY = pl.BlockSpec(memory_space=pl.ANY)
INSIDE = pl.BlockSpec(memory_space=pltpu.VMEM)
SCALARS = pl.BlockSpec(memory_space=pltpu.SMEM)
DMA = pltpu.SemaphoreType.DMA


def begin(src, dst, sem):
    copy = pltpu.make_async_copy(src, dst, sem)
    copy.start()
    return copy


def begin_blocks(src, dst, sems):
    for j in range(NB):
        begin(src.at[j], dst.at[j], sems.at[j])


def shape(s, t):
    return jax.ShapeDtypeStruct(s, t)


def teacher_kernel(feat, protos, expo_o, cols_o, feat_s, protos_s, expo_s, logit_s, cols_s, sem, in_sems, out_sems):
    first = begin(feat, feat_s, sem)
    begin_blocks(protos, protos_s, in_sems)
    first.wait()
    feat_s[...] = unit_rows(feat_s[...])

    @pl.loop(0, NB)
    def _(j):
        pltpu.make_async_copy(protos.at[j], protos_s.at[j], in_sems.at[j]).wait()
        sums = []
        for n in range(BK // DIM):
            logit_s[n] = dot(feat_s[...], unit_rows(protos_s[j, n * DIM : (n + 1) * DIM, :]), NT)
            acc = jnp.zeros((8, DIM), f32)
            for r in range(0, ROWS, 64):
                e = jnp.exp2(logit_s[n, r : r + 64, :] * T_EXP2)
                expo_s[j, r : r + 64, n * DIM : (n + 1) * DIM] = e.astype(bf16)
                for q in range(0, 64, 8):
                    acc = acc + e[q : q + 8]
            sums.append(jnp.sum(acc, axis=0, keepdims=True))
        cols_s[pl.ds(j, 1), :] = jnp.concatenate(sums, axis=1)
        pltpu.make_async_copy(expo_s.at[j], expo_o.at[j], out_sems.at[j]).start()

    cols_o[...] = jnp.broadcast_to(cols_s[...].astype(bf16)[None], cols_o.shape)
    for j in range(NB):
        pltpu.make_async_copy(expo_s.at[j], expo_o.at[j], out_sems.at[j]).wait()


def teacher(feat, protos):
    return call(
        teacher_kernel,
        [ANY, ANY],
        [ANY, INSIDE],
        [shape((NB, ROWS, BK), bf16), shape((NX * NZ, NB, BK), bf16)],
        [
            pltpu.VMEM((ROWS, DIM), bf16),
            pltpu.VMEM((NB, BK, DIM), bf16),
            pltpu.VMEM((NB, ROWS, BK), bf16),
            pltpu.VMEM((BK // DIM, ROWS, DIM), f32),
            pltpu.VMEM((NB, BK), f32),
            DMA,
            DMA((NB,)),
            DMA((NB,)),
        ],
        2 * ROWS * COLS * DIM,
        ROWS * COLS * 2 + COLS * DIM * 2,
        "teacher",
    )(feat, protos.reshape(NB, BK, DIM))


def student_kernel(
    feat, protos, dirs_o, tot_o, mix_o, feat_s, protos_s, dirs_s, logit_s, exp_s, tot_s, sem, in_sems, out_sems
):
    first = begin(feat, feat_s, sem)
    begin_blocks(protos, protos_s, in_sems)
    first.wait()
    feat_s[...] = unit_rows(feat_s[...])
    tot_s[...] = jnp.zeros_like(tot_s)
    mix_o[...] = jnp.zeros_like(mix_o)

    @pl.loop(0, NB, unroll=2)
    def _(j):
        pltpu.make_async_copy(protos.at[j], protos_s.at[j], in_sems.at[j]).wait()
        for n in range(BK // DIM):
            part = slice(n * DIM, (n + 1) * DIM)
            dirs = unit_rows(protos_s[j, part, :])
            dirs_s[j, part, :] = dirs
            logit_s[n] = dot(feat_s[...], dirs, NT)
            for r in range(0, ROWS, 64):
                e = jnp.exp2(logit_s[n, r : r + 64, :] * S_EXP2)
                exp_s[r : r + 64, part] = e.astype(bf16)
                tot_s[r : r + 64, :] += lane_fold(e)
        mix_o[...] += dot(exp_s[...], dirs_s[j], NN)
        pltpu.make_async_copy(dirs_s.at[j], dirs_o.at[j], out_sems.at[j]).start()

    tot_o[...] = rows4(to_lanes(tot_s[...]))
    for j in range(NB):
        pltpu.make_async_copy(dirs_s.at[j], dirs_o.at[j], out_sems.at[j]).wait()


def student(feat, protos):
    return call(
        student_kernel,
        [ANY, ANY],
        [ANY, INSIDE, INSIDE],
        [shape((NB, BK, DIM), bf16), shape((4, 128), f32), shape((ROWS, DIM), f32)],
        [
            pltpu.VMEM((ROWS, DIM), bf16),
            pltpu.VMEM((NB, BK, DIM), bf16),
            pltpu.VMEM((NB, BK, DIM), bf16),
            pltpu.VMEM((BK // DIM, ROWS, DIM), f32),
            pltpu.VMEM((ROWS, BK), bf16),
            pltpu.VMEM((ROWS, 128), f32),
            DMA,
            DMA((NB,)),
            DMA((NB,)),
        ],
        4 * ROWS * COLS * DIM,
        COLS * DIM * 4,
        "student",
    )(feat, protos.reshape(NB, BK, DIM))


def col_scale(got):
    return 1.0 / (PROTOS * jnp.sum(got[...].astype(f32), axis=0))


def scaled_rows(expo, col, acc_s, j):
    c = col[pl.ds(j, 1), :]
    cs = [c[:, g * 128 : (g + 1) * 128] for g in range(BK // 128)]
    for r in range(0, ROWS, 32):
        acc = acc_s[r : r + 32, :]
        for g in range(BK // 128):
            acc = acc + expo[j, r : r + 32, g * 128 : (g + 1) * 128].astype(f32) * cs[g]
        acc_s[r : r + 32, :] = acc


def row_sums(expo, got, col, acc_s):
    acc_s[...] = jnp.zeros_like(acc_s)
    col[...] = col_scale(got[:, :, :BK])

    @pl.loop(0, NB)
    def _(j):
        scaled_rows(expo, col, acc_s, j)

    return rows4(to_lanes(acc_s[...]))


def row_kernel(expo, got, tot, rows_o, col_s, acc_s, tot_s, sem):
    first = begin(tot, tot_s, sem)
    part = row_sums(expo, got, col_s, acc_s)
    first.wait()
    part = jnp.concatenate([part, tot_s[...]], axis=0)
    rows_o[...] = jnp.broadcast_to(part[None], rows_o.shape)


def row_pass(held, got, tot):
    return call(
        row_kernel,
        [INSIDE, INSIDE, ANY],
        INSIDE,
        shape((NY * NC, 8, 128), f32),
        [pltpu.VMEM((NB, BK), f32), pltpu.VMEM((ROWS, 128), f32), pltpu.VMEM((4, 128), f32), DMA],
        2 * ROWS * COLS,
        1 << 16,
        "row_pass",
        SMALL,
    )(pltpu.with_memory_space_constraint(held, pltpu.VMEM), got, tot)


def row_last_kernel(expo, got, rows_o, col_o, acc_s):
    part = row_sums(expo, got, col_o, acc_s)
    rows_o[...] = jnp.broadcast_to(part[None], rows_o.shape)


def row_last(held, got):
    return call(
        row_last_kernel,
        [INSIDE, INSIDE],
        [INSIDE, INSIDE],
        [shape((NZ * NY * NC, 4, 128), f32), shape((NB, BK), f32)],
        [pltpu.VMEM((ROWS, 128), f32)],
        2 * ROWS * COLS,
        1 << 16,
        "row_last",
        SMALL,
    )(pltpu.with_memory_space_constraint(held, pltpu.VMEM), got)


def col_kernel(expo, got, cols_o, tot_o, scale_s, cols_s):
    total = jnp.sum(got[...], axis=0)
    scale_s[...] = jnp.broadcast_to(1.0 / (BATCH * lanes512(total[:4])), (128, ROWS)).T

    @pl.loop(0, NB)
    def _(j):
        accs = [jnp.zeros((8, 128), f32)] * (BK // 128)
        for r in range(0, ROWS, 32):
            scale = scale_s[r : r + 32, :]
            for g in range(BK // 128):
                t = expo[j, r : r + 32, g * 128 : (g + 1) * 128].astype(f32) * scale
                accs[g] = accs[g] + ((t[0:8] + t[8:16]) + (t[16:24] + t[24:32]))
        cols_s[pl.ds(j, 1), :] = jnp.concatenate(
            [jnp.sum(a, axis=0, keepdims=True) for a in accs], axis=1
        )

    cols_o[...] = jnp.broadcast_to(cols_s[...].astype(bf16)[None], cols_o.shape)
    hi = total[4:].astype(bf16).astype(f32)
    tot_o[...] = jnp.concatenate([hi, total[4:] - hi], axis=0).astype(bf16)


def col_pass(held, got, copies):
    return call(
        col_kernel,
        [INSIDE, INSIDE],
        [INSIDE, INSIDE],
        [shape((copies, NB, BK), bf16), shape((8, 128), bf16)],
        [pltpu.VMEM((ROWS, 128), f32), pltpu.VMEM((NB, BK), f32)],
        2 * ROWS * COLS,
        1 << 20,
        "col_pass",
        SMALL,
    )(pltpu.with_memory_space_constraint(held, pltpu.VMEM), got)


def mix_kernel(expo, col, dirs, feat, mix_o, cross_o, expo_s, dirs_s, feat_s, w_s, sem, sems):
    for j in range(NB):
        begin(expo.at[j], expo_s.at[j], sems.at[0, j])
        begin(dirs.at[j], dirs_s.at[j], sems.at[1, j])
    first = begin(feat, feat_s, sem)
    mix_o[...] = jnp.zeros_like(mix_o)

    @pl.loop(0, NB)
    def _(j):
        pltpu.make_async_copy(expo.at[j], expo_s.at[j], sems.at[0, j]).wait()
        c = col[pl.ds(j, 1), :]
        cs = [c[:, g * 128 : (g + 1) * 128] for g in range(BK // 128)]
        for r in range(0, ROWS, 32):
            for g in range(BK // 128):
                part = slice(g * 128, (g + 1) * 128)
                w_s[r : r + 32, part] = (expo_s[j, r : r + 32, part].astype(f32) * cs[g]).astype(bf16)
        pltpu.make_async_copy(dirs.at[j], dirs_s.at[j], sems.at[1, j]).wait()
        mix_o[...] += dot(w_s[...], dirs_s[j], NN)

    first.wait()
    unit = unit_rows(feat_s[...]).astype(f32)
    cross_o[...] = to_lanes(lane_fold(mix_o[...] * unit)) / 0.1


def mix_pass(expo, col, dirs, feat):
    return call(
        mix_kernel,
        [ANY, INSIDE, ANY, ANY],
        [INSIDE, INSIDE],
        [shape((ROWS, DIM), f32), shape((1, ROWS), f32)],
        [
            pltpu.VMEM((NB, ROWS, BK), bf16),
            pltpu.VMEM((NB, BK, DIM), bf16),
            pltpu.VMEM((ROWS, DIM), bf16),
            pltpu.VMEM((ROWS, BK), bf16),
            DMA,
            DMA((2, NB)),
        ],
        2 * ROWS * COLS * DIM,
        ROWS * COLS * 2 + COLS * DIM * 2,
        "mix_pass",
    )(expo, col, dirs, feat)


def early_kernel(*refs):
    pos, mine, other = refs[0], refs[1 : 1 + NZ], refs[1 + NZ : 1 + 2 * NZ]
    (t_protos, s_dirs, got, rows_o, dirs_o, grad_o,
     raw_s, rows_s, t_s, s_s, got_s, d_s, small, sems, outs) = refs[1 + 2 * NZ :]
    z, core = pos[0], pos[1]
    for k in range(NZ):
        begin(mine[k], raw_s.at[k, core], sems.at[0, k])
        begin(other[k], raw_s.at[k, 1 - core], sems.at[1, k])
        if k == 0:
            first = [begin(t_protos.at[i, z], t_s.at[pl.ds(i * DIM, DIM)], small.at[i]) for i in range(NX)]
            first += [begin(s_dirs.at[i, z], s_s.at[pl.ds(i * DIM, DIM)], small.at[NX + i]) for i in range(NX)]
            first.append(begin(got, got_s, small.at[2 * NX]))
    grad_o[...] = jnp.zeros_like(grad_o)
    for copy in first:
        copy.wait()
    dirs_o[...] = unit_rows(t_s[...])

    @pl.loop(0, NZ)
    def _(k):
        pltpu.make_async_copy(mine[0], raw_s.at[k, core], sems.at[0, k]).wait()
        pltpu.make_async_copy(other[0], raw_s.at[k, 1 - core], sems.at[1, k]).wait()
        total = got_s[pos[3 + k]].astype(f32)[:, BK:]
        scale = FACTOR / lanes512(total[:4] + total[4:])
        half = ROWS // NC
        for h in range(NC):
            part = slice(h * half, (h + 1) * half)
            rows_s[k, part, :DIM] = unit_rows(raw_s[k, h, :, :DIM])
            rows_s[k, part, DIM:] = unit_rows(raw_s[k, h, :, DIM:])
        pltpu.make_async_copy(rows_s.at[k], rows_o.at[k], outs.at[k]).start()
        s_rows = rows_s[k, :, DIM:]
        d_s[...] = (jnp.exp2(dot(s_s[...], s_rows, NT) * S_EXP2) * scale).astype(bf16)
        grad_o[...] += dot(d_s[...], s_rows, NN)

    for k in range(NZ):
        pltpu.make_async_copy(rows_s.at[k], rows_o.at[k], outs.at[k]).wait()


def early(pos, mine, other, t_protos, s_dirs, got):
    n, half = NX * DIM, ROWS // NC
    return call(
        early_kernel,
        [SCALARS] + [ANY] * (2 * NZ + 3),
        [ANY, INSIDE, INSIDE],
        [shape((NZ, ROWS, 2 * DIM), bf16), shape((n, DIM), bf16), shape((n, DIM), f32)],
        [
            pltpu.VMEM((NZ, NC, half, 2 * DIM), bf16),
            pltpu.VMEM((NZ, ROWS, 2 * DIM), bf16),
            pltpu.VMEM((n, DIM), bf16),
            pltpu.VMEM((n, DIM), bf16),
            pltpu.VMEM(got.shape, bf16),
            pltpu.VMEM((n, ROWS), bf16),
            DMA((2 * NX + 1,)),
            DMA((2, NZ)),
            DMA((NZ,)),
        ],
        4 * ROWS * COLS * DIM,
        ROWS * COLS,
        "early",
    )(pos, *mine, *other, t_protos, s_dirs, got)


def down_rows(v):
    return jnp.broadcast_to(v, (128, v.shape[1])).T


def scale_rows(m, scale):
    return jnp.concatenate([m[:, g : g + 128] * scale for g in range(0, m.shape[1], 128)], axis=1)


def grad_kernel(
    pos, dirs, rows, stat, got, student_part, col, s_mix, t_mix, cross,
    own_o, next1_o, next2_o, next3_o, keep_o, give_o, line_o,
    rows_s, got_s, dirs_s, part_s, acc_s, s_mix_s, t_mix_s, small, sems,
):
    z, core, x = pos[0], pos[1], pos[2]
    first = [begin(dirs, dirs_s, small.at[1])]
    for k in range(NZ):
        begin(rows.at[k], rows_s.at[k], sems.at[k])
    second = [
        begin(got.at[pl.ds(z, 1)], got_s, small.at[2]),
        begin(s_mix, s_mix_s, small.at[3]),
        begin(t_mix, t_mix_s, small.at[4]),
        begin(student_part, part_s, small.at[5]),
    ]
    acc_s[...] = jnp.zeros_like(acc_s)
    for copy in first:
        copy.wait()

    @pl.loop(0, NZ, unroll=2)
    def _(k):
        total = jnp.sum(stat[pos[3 + k]], axis=0)
        scale = down_rows(FACTOR / lanes512(total))
        pltpu.make_async_copy(rows.at[k], rows_s.at[k], sems.at[k]).wait()
        expo = jnp.exp2(dot(dirs_s[...], rows_s[k, :, :DIM], NT) * T_EXP2).astype(bf16)
        r = scale_rows(rows_s[k, :, DIM:].astype(f32), scale).astype(bf16)
        acc_s[...] += dot(expo, r, NN)

    for copy in second:
        copy.wait()
    for d in range(NX):
        i = lax.rem(x + d, NX)
        c = col[pl.ds(2 * i + z // 4, 1), :]
        c = sum(jnp.where(lax.rem(z, 4) == q, c[:, q * DIM : (q + 1) * DIM], 0.0) for q in range(4))
        part = pl.ds(pl.multiple_of(i * DIM, DIM), DIM)
        block = part_s[part, :] - scale_rows(acc_s[part, :], down_rows(c))
        if d == 0:
            own_o[...] = block
        else:
            (next1_o, next2_o, next3_o)[d - 1][...] = block.astype(bf16)

    row_total = lanes512(jnp.sum(stat[z], axis=0))
    total = got_s[0].astype(f32)[:, BK:]
    total = lanes512(total[:4] + total[4:])
    s_mix_s[...] = scale_rows(s_mix_s[...], down_rows(FACTOR / total)) - scale_rows(
        t_mix_s[...], down_rows(FACTOR / row_total)
    )
    half = ROWS // NC
    keep_o[:half, :] = s_mix_s[pl.ds(pl.multiple_of(core * half, half), half), :]
    give_o[:half, :] = s_mix_s[pl.ds(pl.multiple_of((1 - core) * half, half), half), :].astype(bf16)
    loss = cross[...] / row_total
    low, high = loss[:, :half], loss[:, half:]
    away = jnp.where(core == 0, high, low)
    hi = away.astype(bf16).astype(f32)
    zeros = jnp.zeros((14, DIM), f32)
    give_o[half:, :] = jnp.concatenate([hi, away - hi, zeros], axis=0).astype(bf16)
    keep_o[half:, :] = jnp.concatenate([jnp.where(core == 0, low, high), zeros[:7]], axis=0)
    line_o[...] = jnp.log(total)


def proto_part(pos, dirs, rows, stat, got, student_part, col, s_mix, t_mix, cross):
    n, half = NX * DIM, ROWS // NC
    return call(
        grad_kernel,
        [SCALARS, ANY, ANY, INSIDE, ANY, ANY, INSIDE, ANY, ANY, INSIDE],
        [INSIDE] * 7,
        [
            shape((DIM, DIM), f32),
            shape((DIM, DIM), bf16),
            shape((DIM, DIM), bf16),
            shape((DIM, DIM), bf16),
            shape((half + 8, DIM), f32),
            shape((half + 16, DIM), bf16),
            shape((1, ROWS), f32),
        ],
        [
            pltpu.VMEM((NZ, ROWS, 2 * DIM), bf16),
            pltpu.VMEM((1,) + got.shape[1:], bf16),
            pltpu.VMEM((n, DIM), bf16),
            pltpu.VMEM((n, DIM), f32),
            pltpu.VMEM((n, DIM), f32),
            pltpu.VMEM((ROWS, DIM), f32),
            pltpu.VMEM((ROWS, DIM), f32),
            DMA((6,)),
            DMA((NZ,)),
        ],
        4 * ROWS * COLS * DIM,
        ROWS * COLS,
        "proto_part",
        MIDDLE,
    )(pos, dirs, rows, stat, got, student_part, col, s_mix, t_mix, cross)


def gather(a, axes):
    return lax.all_to_all(a, axes, 0, 0)


def swap_core(a):
    return lax.ppermute(a, "c", [(0, 1), (1, 0)])


def shift(a, axis, by):
    n = lax.axis_size(axis)
    return lax.ppermute(a, axis, [(i, (i + by) % n) for i in range(n)])


OFFSETS = (0, -1, 1, -2, 2, -3, 3, -4)


def packed(terms, loss):
    hi = lax.reduce_precision(loss, 8, 7)
    tail = jnp.concatenate([hi, loss - hi, jnp.zeros((14, DIM), f32)], axis=0)
    return jnp.concatenate([terms, tail], axis=0).astype(bf16)


def unpacked(a):
    a = a.astype(f32)
    n = a.shape[0] - 16
    return a[:n], a[n : n + 1] + a[n + 1 : n + 2]


def around(a, axis):
    one, two, three = [shift(a, axis, d).astype(f32) for d in (1, 2, 3)]
    return (a.astype(f32) + two) + (one + three)


def local(teacher_feat, student_feat, teacher_protos, student_protos):
    z = lax.axis_index("z")
    core = lax.axis_index("c")
    half = ROWS // NC
    together = lax.optimization_barrier

    def my_half(a):
        return lax.dynamic_slice_in_dim(a, core * half, half, 0)

    order = (z + jnp.array(OFFSETS, jnp.int32)) % NZ
    pos = jnp.concatenate([jnp.stack([z, core, lax.axis_index("x")]), order]).astype(jnp.int32)

    b0 = jnp.concatenate([my_half(teacher_feat), my_half(student_feat)], axis=1)
    u1, d1 = shift(b0, "z", 1), shift(b0, "z", -1)
    expo, cols = teacher(teacher_feat, teacher_protos)
    cols, u1, d1 = together((cols, u1, d1))

    u2, d2 = shift(u1, "z", 1), shift(d1, "z", -1)
    o0, ou1, od1 = swap_core(b0), swap_core(u1), swap_core(d1)
    got = gather(cols, ("x", "z"))
    s_dirs, tot, s_mix = student(student_feat, student_protos)
    got, u2, d2, o0, ou1, od1, tot = together((got, u2, d2, o0, ou1, od1, tot))

    u3, d3 = shift(u2, "z", 1), shift(d2, "z", -1)
    ou2, od2 = swap_core(u2), swap_core(d2)
    rows = row_pass(expo, got, tot)
    rows, u3, d3, ou2, od2 = together((rows, u3, d3, ou2, od2))
    u4 = shift(u3, "z", 1)
    got = gather(rows, ("y", "c"))
    got, u4 = together((got, u4))

    cols, tots = col_pass(expo, got, 1)
    cols = around(cols[0], "x").astype(bf16)
    cols = jnp.concatenate([cols, tots], axis=1)
    got2 = gather(jnp.broadcast_to(cols[None], (NZ,) + cols.shape), "z")

    got2, u3, d3, u4 = together((got2, u3, d3, u4))
    ou3, od3, ou4 = swap_core(u3), swap_core(d3), swap_core(u4)
    rows = row_pass(expo, got2, tot)
    rows, ou3, od3, ou4 = together((rows, ou3, od3, ou4))
    got = gather(rows, ("y", "c"))
    cols, _ = col_pass(expo, got, NX * NZ)

    got = gather(cols, ("x", "z"))
    rows_c, dirs_c, student_part = early(
        pos,
        [b0, u1, d1, u2, d2, u3, d3, u4],
        [o0, ou1, od1, ou2, od2, ou3, od3, ou4],
        teacher_protos.reshape(NX, NZ, DIM, DIM),
        s_dirs.reshape(NX, NZ, DIM, DIM),
        got2,
    )
    got, student_part = together((got, student_part))

    rows, col = row_last(expo, got)
    rows, col = together((rows, col))
    stat = gather(rows, ("z", "y", "c")).reshape(NZ, NY * NC, 4, 128)
    t_mix, cross = mix_pass(expo, col, s_dirs, student_feat)
    stat, t_mix, cross = together((stat, t_mix, cross))
    own, next1, next2, next3, keep, give, log_total = proto_part(
        pos, dirs_c, rows_c, stat, got2, student_part, col, s_mix, t_mix, cross
    )
    arrived = [shift(a, "x", d).astype(f32) for a, d in ((next1, 1), (next2, 2), (next3, 3))]
    proto_grad = ((own + arrived[0]) + (arrived[1] + arrived[2])).astype(bf16)

    terms, loss = unpacked(swap_core(give))
    mine = packed(keep[:half] + terms, keep[half : half + 1] + loss)
    terms, loss = unpacked(mine)
    away = [unpacked(shift(mine, "y", d)) for d in (1, 2, 3)]
    terms = (terms + away[1][0]) + (away[0][0] + away[2][0])
    loss = (loss + away[1][1]) + (away[0][1] + away[2][1])
    done = packed(terms, loss)
    there = swap_core(done)
    low, low_loss = unpacked(jnp.where(core == 0, done, there))
    high, high_loss = unpacked(jnp.where(core == 0, there, done))
    feature_grad = jnp.concatenate([low, high], axis=0).astype(bf16)
    row_loss = (log_total - jnp.concatenate([low_loss, high_loss], axis=1)).reshape(ROWS)
    return row_loss, feature_grad, proto_grad


def solution(mesh):
    fine = Mesh(mesh.devices.reshape(NX, NZ, NY, NC), ("x", "z", "y", "c"))
    rows, protos = P(("x", "z"), None), P(("y", "c"), None)
    return jax.shard_map(
        local,
        mesh=fine,
        in_specs=(rows, rows, protos, protos),
        out_specs=(P(("x", "z")), rows, P(("y", "c", "x", "z"), None)),
        check_vma=False,
    )
```

```python
import math

import jax
import jax.numpy as jnp
from jax import lax
from jax.experimental import pallas as pl
from jax.experimental.pallas import tpu as pltpu
from jax.sharding import Mesh, PartitionSpec as P

f32 = jnp.float32
bf16 = jnp.bfloat16

NX, NZ, NY, NC = 4, 8, 4, 2
DIM = 256
PROTOS = 65536
BATCH = 16384
ROWS = BATCH // (NX * NZ)
COLS = PROTOS // (NY * NC)
BK = 1024
NB = COLS // BK
T_EXP2 = math.log2(math.e) / 0.07
S_EXP2 = math.log2(math.e) / 0.1
FACTOR = PROTOS / (BATCH * 0.1)
VMEM = 60 * 1024 * 1024
SMALL = 24 * 1024 * 1024
MIDDLE = 48 * 1024 * 1024

NT = (((1,), (1,)), ((), ()))
NN = (((1,), (0,)), ((), ()))


def dot(a, b, dims):
    return lax.dot_general(a, b, dims, preferred_element_type=f32)


def unit_rows(x):
    xf = x.astype(f32)
    return (xf * lax.rsqrt(jnp.sum(xf * xf, axis=1, keepdims=True) + 1e-06)).astype(bf16)


def lane_fold(m):
    acc = m[:, :128]
    for i in range(1, m.shape[1] // 128):
        acc = acc + m[:, i * 128 : (i + 1) * 128]
    return acc


def to_lanes(acc):
    return jnp.sum(acc.T, axis=0, keepdims=True)


def rows4(v):
    return jnp.concatenate([v[:, i * 128 : (i + 1) * 128] for i in range(4)], axis=0)


def lanes512(m):
    return jnp.concatenate([m[i : i + 1] for i in range(4)], axis=1)


def call(kernel, ins, outs, out_shape, scratch, flops, nbytes, name, limit=VMEM):
    return pl.pallas_call(
        kernel,
        in_specs=ins,
        out_specs=outs,
        out_shape=out_shape,
        scratch_shapes=scratch,
        compiler_params=pltpu.CompilerParams(vmem_limit_bytes=limit),
        cost_estimate=pl.CostEstimate(flops=flops, bytes_accessed=nbytes, transcendentals=0),
        name=name,
    )


ANY = pl.BlockSpec(memory_space=pl.ANY)
OUTSIDE = pl.BlockSpec(memory_space=pltpu.HBM)
INSIDE = pl.BlockSpec(memory_space=pltpu.VMEM)
SCALARS = pl.BlockSpec(memory_space=pltpu.SMEM)
DMA = pltpu.SemaphoreType.DMA


def outside(a):
    return pltpu.with_memory_space_constraint(a, pltpu.HBM)


def begin(src, dst, sem):
    copy = pltpu.make_async_copy(src, dst, sem)
    copy.start()
    return copy


def begin_blocks(src, dst, sems):
    for j in range(NB):
        begin(src.at[j], dst.at[j], sems.at[j])


def shape(s, t):
    return jax.ShapeDtypeStruct(s, t)


def teacher_kernel(feat, protos, expo_o, cols_o, feat_s, protos_s, expo_s, logit_s, cols_s, sem, in_sems, out_sems):
    first = begin(feat, feat_s, sem)
    begin_blocks(protos, protos_s, in_sems)
    first.wait()
    feat_s[...] = unit_rows(feat_s[...])

    @pl.loop(0, NB)
    def _(j):
        pltpu.make_async_copy(protos.at[j], protos_s.at[j], in_sems.at[j]).wait()
        sums = []
        for n in range(BK // DIM):
            logit_s[n] = dot(feat_s[...], unit_rows(protos_s[j, n * DIM : (n + 1) * DIM, :]), NT)
            acc = jnp.zeros((8, DIM), f32)
            for r in range(0, ROWS, 64):
                e = jnp.exp2(logit_s[n, r : r + 64, :] * T_EXP2)
                expo_s[j, r : r + 64, n * DIM : (n + 1) * DIM] = e.astype(bf16)
                for q in range(0, 64, 8):
                    acc = acc + e[q : q + 8]
            sums.append(jnp.sum(acc, axis=0, keepdims=True))
        cols_s[pl.ds(j, 1), :] = jnp.concatenate(sums, axis=1)
        pltpu.make_async_copy(expo_s.at[j], expo_o.at[j], out_sems.at[j]).start()

    cols_o[...] = jnp.broadcast_to(cols_s[...].astype(bf16)[None], cols_o.shape)
    for j in range(NB):
        pltpu.make_async_copy(expo_s.at[j], expo_o.at[j], out_sems.at[j]).wait()


def teacher(feat, protos):
    return call(
        teacher_kernel,
        [ANY, ANY],
        [ANY, INSIDE],
        [shape((NB, ROWS, BK), bf16), shape((NX * NZ, NB, BK), bf16)],
        [
            pltpu.VMEM((ROWS, DIM), bf16),
            pltpu.VMEM((NB, BK, DIM), bf16),
            pltpu.VMEM((NB, ROWS, BK), bf16),
            pltpu.VMEM((BK // DIM, ROWS, DIM), f32),
            pltpu.VMEM((NB, BK), f32),
            DMA,
            DMA((NB,)),
            DMA((NB,)),
        ],
        2 * ROWS * COLS * DIM,
        ROWS * COLS * 2 + COLS * DIM * 2,
        "teacher",
    )(feat, protos.reshape(NB, BK, DIM))


def student_kernel(
    feat, protos, dirs_o, tot_o, mix_o, feat_s, protos_s, dirs_s, logit_s, exp_s, tot_s, sem, in_sems, out_sems
):
    first = begin(feat, feat_s, sem)
    begin_blocks(protos, protos_s, in_sems)
    first.wait()
    feat_s[...] = unit_rows(feat_s[...])
    tot_s[...] = jnp.zeros_like(tot_s)
    mix_o[...] = jnp.zeros_like(mix_o)

    @pl.loop(0, NB, unroll=2)
    def _(j):
        pltpu.make_async_copy(protos.at[j], protos_s.at[j], in_sems.at[j]).wait()
        for n in range(BK // DIM):
            part = slice(n * DIM, (n + 1) * DIM)
            dirs = unit_rows(protos_s[j, part, :])
            dirs_s[j, part, :] = dirs
            logit_s[n] = dot(feat_s[...], dirs, NT)
            for r in range(0, ROWS, 64):
                e = jnp.exp2(logit_s[n, r : r + 64, :] * S_EXP2)
                exp_s[r : r + 64, part] = e.astype(bf16)
                tot_s[r : r + 64, :] += lane_fold(e)
        mix_o[...] += dot(exp_s[...], dirs_s[j], NN)
        pltpu.make_async_copy(dirs_s.at[j], dirs_o.at[j], out_sems.at[j]).start()

    tot_o[...] = rows4(to_lanes(tot_s[...]))
    for j in range(NB):
        pltpu.make_async_copy(dirs_s.at[j], dirs_o.at[j], out_sems.at[j]).wait()


def student(feat, protos):
    return call(
        student_kernel,
        [ANY, ANY],
        [ANY, INSIDE, INSIDE],
        [shape((NB, BK, DIM), bf16), shape((4, 128), f32), shape((ROWS, DIM), f32)],
        [
            pltpu.VMEM((ROWS, DIM), bf16),
            pltpu.VMEM((NB, BK, DIM), bf16),
            pltpu.VMEM((NB, BK, DIM), bf16),
            pltpu.VMEM((BK // DIM, ROWS, DIM), f32),
            pltpu.VMEM((ROWS, BK), bf16),
            pltpu.VMEM((ROWS, 128), f32),
            DMA,
            DMA((NB,)),
            DMA((NB,)),
        ],
        4 * ROWS * COLS * DIM,
        COLS * DIM * 4,
        "student",
    )(feat, protos.reshape(NB, BK, DIM))


def col_scale(got):
    return 1.0 / (PROTOS * jnp.sum(got[...].astype(f32), axis=0))


def scaled_rows(expo, col, acc_s, j):
    c = col[pl.ds(j, 1), :]
    cs = [c[:, g * 128 : (g + 1) * 128] for g in range(BK // 128)]
    for r in range(0, ROWS, 32):
        acc = acc_s[r : r + 32, :]
        for g in range(BK // 128):
            acc = acc + expo[j, r : r + 32, g * 128 : (g + 1) * 128].astype(f32) * cs[g]
        acc_s[r : r + 32, :] = acc


def row_sums(expo, got, col, acc_s):
    acc_s[...] = jnp.zeros_like(acc_s)
    col[...] = col_scale(got[:, :, :BK])

    @pl.loop(0, NB)
    def _(j):
        scaled_rows(expo, col, acc_s, j)

    return rows4(to_lanes(acc_s[...]))


def row_kernel(expo, got, tot, rows_o, col_s, acc_s, tot_s, sem):
    first = begin(tot, tot_s, sem)
    part = row_sums(expo, got, col_s, acc_s)
    first.wait()
    part = jnp.concatenate([part, tot_s[...]], axis=0)
    rows_o[...] = jnp.broadcast_to(part[None], rows_o.shape)


def row_pass(held, got, tot):
    return call(
        row_kernel,
        [INSIDE, INSIDE, OUTSIDE],
        INSIDE,
        shape((NY * NC, 8, 128), f32),
        [pltpu.VMEM((NB, BK), f32), pltpu.VMEM((ROWS, 128), f32), pltpu.VMEM((4, 128), f32), DMA],
        2 * ROWS * COLS,
        1 << 16,
        "row_pass",
        SMALL,
    )(pltpu.with_memory_space_constraint(held, pltpu.VMEM), got, outside(tot))


def row_last_kernel(expo, got, rows_o, col_o, acc_s):
    part = row_sums(expo, got, col_o, acc_s)
    rows_o[...] = jnp.broadcast_to(part[None], rows_o.shape)


def row_last(held, got):
    return call(
        row_last_kernel,
        [INSIDE, INSIDE],
        [INSIDE, INSIDE],
        [shape((NZ * NY * NC, 4, 128), f32), shape((NB, BK), f32)],
        [pltpu.VMEM((ROWS, 128), f32)],
        2 * ROWS * COLS,
        1 << 16,
        "row_last",
        SMALL,
    )(pltpu.with_memory_space_constraint(held, pltpu.VMEM), got)


def col_kernel(expo, got, cols_o, tot_o, scale_s, cols_s):
    total = jnp.sum(got[...], axis=0)
    scale_s[...] = jnp.broadcast_to(1.0 / (BATCH * lanes512(total[:4])), (128, ROWS)).T

    @pl.loop(0, NB)
    def _(j):
        accs = [jnp.zeros((8, 128), f32)] * (BK // 128)
        for r in range(0, ROWS, 32):
            scale = scale_s[r : r + 32, :]
            for g in range(BK // 128):
                t = expo[j, r : r + 32, g * 128 : (g + 1) * 128].astype(f32) * scale
                accs[g] = accs[g] + ((t[0:8] + t[8:16]) + (t[16:24] + t[24:32]))
        cols_s[pl.ds(j, 1), :] = jnp.concatenate(
            [jnp.sum(a, axis=0, keepdims=True) for a in accs], axis=1
        )

    cols_o[...] = jnp.broadcast_to(cols_s[...].astype(bf16)[None], cols_o.shape)
    hi = total[4:].astype(bf16).astype(f32)
    tot_o[...] = jnp.concatenate([hi, total[4:] - hi], axis=0).astype(bf16)


def col_pass(held, got, copies):
    return call(
        col_kernel,
        [INSIDE, INSIDE],
        [INSIDE, INSIDE],
        [shape((copies, NB, BK), bf16), shape((8, 128), bf16)],
        [pltpu.VMEM((ROWS, 128), f32), pltpu.VMEM((NB, BK), f32)],
        2 * ROWS * COLS,
        1 << 20,
        "col_pass",
        SMALL,
    )(pltpu.with_memory_space_constraint(held, pltpu.VMEM), got)


def mix_kernel(expo, col, dirs, feat, mix_o, cross_o, expo_s, dirs_s, feat_s, w_s, sem, sems):
    for j in range(NB):
        begin(expo.at[j], expo_s.at[j], sems.at[0, j])
        begin(dirs.at[j], dirs_s.at[j], sems.at[1, j])
    first = begin(feat, feat_s, sem)
    mix_o[...] = jnp.zeros_like(mix_o)

    @pl.loop(0, NB)
    def _(j):
        pltpu.make_async_copy(expo.at[j], expo_s.at[j], sems.at[0, j]).wait()
        c = col[pl.ds(j, 1), :]
        cs = [c[:, g * 128 : (g + 1) * 128] for g in range(BK // 128)]
        for r in range(0, ROWS, 32):
            for g in range(BK // 128):
                part = slice(g * 128, (g + 1) * 128)
                w_s[r : r + 32, part] = (expo_s[j, r : r + 32, part].astype(f32) * cs[g]).astype(bf16)
        pltpu.make_async_copy(dirs.at[j], dirs_s.at[j], sems.at[1, j]).wait()
        mix_o[...] += dot(w_s[...], dirs_s[j], NN)

    first.wait()
    unit = unit_rows(feat_s[...]).astype(f32)
    cross_o[...] = to_lanes(lane_fold(mix_o[...] * unit)) / 0.1


def mix_pass(expo, col, dirs, feat):
    return call(
        mix_kernel,
        [ANY, INSIDE, ANY, ANY],
        [INSIDE, INSIDE],
        [shape((ROWS, DIM), f32), shape((1, ROWS), f32)],
        [
            pltpu.VMEM((NB, ROWS, BK), bf16),
            pltpu.VMEM((NB, BK, DIM), bf16),
            pltpu.VMEM((ROWS, DIM), bf16),
            pltpu.VMEM((ROWS, BK), bf16),
            DMA,
            DMA((2, NB)),
        ],
        2 * ROWS * COLS * DIM,
        ROWS * COLS * 2 + COLS * DIM * 2,
        "mix_pass",
    )(expo, col, dirs, feat)


def early_kernel(*refs):
    pos, mine, other = refs[0], refs[1 : 1 + NZ], refs[1 + NZ : 1 + 2 * NZ]
    (t_protos, s_dirs, got, rows_o, dirs_o, grad_o,
     raw_s, rows_s, t_s, s_s, got_s, d_s, small, sems, outs) = refs[1 + 2 * NZ :]
    z, core = pos[0], pos[1]
    for k in range(NZ):
        begin(mine[k], raw_s.at[k, core], sems.at[0, k])
        begin(other[k], raw_s.at[k, 1 - core], sems.at[1, k])
        if k == 0:
            first = [begin(t_protos.at[i, z], t_s.at[pl.ds(i * DIM, DIM)], small.at[i]) for i in range(NX)]
            first += [begin(s_dirs.at[i, z], s_s.at[pl.ds(i * DIM, DIM)], small.at[NX + i]) for i in range(NX)]
            first.append(begin(got, got_s, small.at[2 * NX]))
    grad_o[...] = jnp.zeros_like(grad_o)
    for copy in first:
        copy.wait()
    dirs_o[...] = unit_rows(t_s[...])

    @pl.loop(0, NZ)
    def _(k):
        pltpu.make_async_copy(mine[0], raw_s.at[k, core], sems.at[0, k]).wait()
        pltpu.make_async_copy(other[0], raw_s.at[k, 1 - core], sems.at[1, k]).wait()
        total = got_s[pos[3 + k]].astype(f32)[:, BK:]
        scale = FACTOR / lanes512(total[:4] + total[4:])
        half = ROWS // NC
        for h in range(NC):
            part = slice(h * half, (h + 1) * half)
            rows_s[k, part, :DIM] = unit_rows(raw_s[k, h, :, :DIM])
            rows_s[k, part, DIM:] = unit_rows(raw_s[k, h, :, DIM:])
        pltpu.make_async_copy(rows_s.at[k], rows_o.at[k], outs.at[k]).start()
        s_rows = rows_s[k, :, DIM:]
        d_s[...] = (jnp.exp2(dot(s_s[...], s_rows, NT) * S_EXP2) * scale).astype(bf16)
        grad_o[...] += dot(d_s[...], s_rows, NN)

    for k in range(NZ):
        pltpu.make_async_copy(rows_s.at[k], rows_o.at[k], outs.at[k]).wait()


def early(pos, mine, other, t_protos, s_dirs, got):
    n, half = NX * DIM, ROWS // NC
    return call(
        early_kernel,
        [SCALARS] + [ANY] * (2 * NZ + 3),
        [ANY, INSIDE, INSIDE],
        [shape((NZ, ROWS, 2 * DIM), bf16), shape((n, DIM), bf16), shape((n, DIM), f32)],
        [
            pltpu.VMEM((NZ, NC, half, 2 * DIM), bf16),
            pltpu.VMEM((NZ, ROWS, 2 * DIM), bf16),
            pltpu.VMEM((n, DIM), bf16),
            pltpu.VMEM((n, DIM), bf16),
            pltpu.VMEM(got.shape, bf16),
            pltpu.VMEM((n, ROWS), bf16),
            DMA((2 * NX + 1,)),
            DMA((2, NZ)),
            DMA((NZ,)),
        ],
        4 * ROWS * COLS * DIM,
        ROWS * COLS,
        "early",
    )(pos, *mine, *other, t_protos, s_dirs, got)


def down_rows(v):
    return jnp.broadcast_to(v, (128, v.shape[1])).T


def scale_rows(m, scale):
    return jnp.concatenate([m[:, g : g + 128] * scale for g in range(0, m.shape[1], 128)], axis=1)


def grad_kernel(
    pos, dirs, rows, stat, got, student_part, col, s_mix, t_mix, cross,
    own_o, next1_o, next2_o, next3_o, keep_o, give_o, line_o,
    rows_s, got_s, dirs_s, part_s, acc_s, s_mix_s, t_mix_s, cross_s, small, sems,
):
    z, core, x = pos[0], pos[1], pos[2]
    first = [begin(dirs, dirs_s, small.at[1])]
    for k in range(NZ):
        begin(rows.at[k], rows_s.at[k], sems.at[k])
    second = [
        begin(got.at[pl.ds(z, 1)], got_s, small.at[2]),
        begin(s_mix, s_mix_s, small.at[3]),
        begin(t_mix, t_mix_s, small.at[4]),
        begin(cross, cross_s, small.at[0]),
        begin(student_part, part_s, small.at[5]),
    ]
    acc_s[...] = jnp.zeros_like(acc_s)
    for copy in first:
        copy.wait()

    @pl.loop(0, NZ, unroll=2)
    def _(k):
        total = jnp.sum(stat[pos[3 + k]], axis=0)
        scale = down_rows(FACTOR / lanes512(total))
        pltpu.make_async_copy(rows.at[k], rows_s.at[k], sems.at[k]).wait()
        expo = jnp.exp2(dot(dirs_s[...], rows_s[k, :, :DIM], NT) * T_EXP2).astype(bf16)
        r = scale_rows(rows_s[k, :, DIM:].astype(f32), scale).astype(bf16)
        acc_s[...] += dot(expo, r, NN)

    for copy in second:
        copy.wait()
    for d in range(NX):
        i = lax.rem(x + d, NX)
        c = col[pl.ds(2 * i + z // 4, 1), :]
        c = sum(jnp.where(lax.rem(z, 4) == q, c[:, q * DIM : (q + 1) * DIM], 0.0) for q in range(4))
        part = pl.ds(pl.multiple_of(i * DIM, DIM), DIM)
        block = part_s[part, :] - scale_rows(acc_s[part, :], down_rows(c))
        if d == 0:
            own_o[...] = block
        else:
            (next1_o, next2_o, next3_o)[d - 1][...] = block.astype(bf16)

    row_total = lanes512(jnp.sum(stat[z], axis=0))
    total = got_s[0].astype(f32)[:, BK:]
    total = lanes512(total[:4] + total[4:])
    s_mix_s[...] = scale_rows(s_mix_s[...], down_rows(FACTOR / total)) - scale_rows(
        t_mix_s[...], down_rows(FACTOR / row_total)
    )
    half = ROWS // NC
    keep_o[:half, :] = s_mix_s[pl.ds(pl.multiple_of(core * half, half), half), :]
    give_o[:half, :] = s_mix_s[pl.ds(pl.multiple_of((1 - core) * half, half), half), :].astype(bf16)
    loss = cross_s[...] / row_total
    low, high = loss[:, :half], loss[:, half:]
    away = jnp.where(core == 0, high, low)
    hi = away.astype(bf16).astype(f32)
    zeros = jnp.zeros((14, DIM), f32)
    give_o[half:, :] = jnp.concatenate([hi, away - hi, zeros], axis=0).astype(bf16)
    keep_o[half:, :] = jnp.concatenate([jnp.where(core == 0, low, high), zeros[:7]], axis=0)
    line_o[...] = jnp.log(total)


def proto_part(pos, dirs, rows, stat, got, student_part, col, s_mix, t_mix, cross):
    n, half = NX * DIM, ROWS // NC
    return call(
        grad_kernel,
        [SCALARS, ANY, ANY, INSIDE, ANY, ANY, INSIDE, ANY, OUTSIDE, OUTSIDE],
        [INSIDE] * 7,
        [
            shape((DIM, DIM), f32),
            shape((DIM, DIM), bf16),
            shape((DIM, DIM), bf16),
            shape((DIM, DIM), bf16),
            shape((half + 8, DIM), f32),
            shape((half + 16, DIM), bf16),
            shape((1, ROWS), f32),
        ],
        [
            pltpu.VMEM((NZ, ROWS, 2 * DIM), bf16),
            pltpu.VMEM((1,) + got.shape[1:], bf16),
            pltpu.VMEM((n, DIM), bf16),
            pltpu.VMEM((n, DIM), f32),
            pltpu.VMEM((n, DIM), f32),
            pltpu.VMEM((ROWS, DIM), f32),
            pltpu.VMEM((ROWS, DIM), f32),
            pltpu.VMEM((1, ROWS), f32),
            DMA((6,)),
            DMA((NZ,)),
        ],
        4 * ROWS * COLS * DIM,
        ROWS * COLS,
        "proto_part",
        MIDDLE,
    )(pos, dirs, rows, stat, got, student_part, col, s_mix, outside(t_mix), outside(cross))


def gather(a, axes):
    return lax.all_to_all(a, axes, 0, 0)


def swap_core(a):
    return lax.ppermute(a, "c", [(0, 1), (1, 0)])


def shift(a, axis, by):
    n = lax.axis_size(axis)
    return lax.ppermute(a, axis, [(i, (i + by) % n) for i in range(n)])


OFFSETS = (0, -1, 1, -2, 2, -3, 3, -4)


def packed(terms, loss):
    hi = lax.reduce_precision(loss, 8, 7)
    tail = jnp.concatenate([hi, loss - hi, jnp.zeros((14, DIM), f32)], axis=0)
    return jnp.concatenate([terms, tail], axis=0).astype(bf16)


def unpacked(a):
    a = a.astype(f32)
    n = a.shape[0] - 16
    return a[:n], a[n : n + 1] + a[n + 1 : n + 2]


def around(a, axis):
    one, two, three = [shift(a, axis, d).astype(f32) for d in (1, 2, 3)]
    return (a.astype(f32) + two) + (one + three)


def local(teacher_feat, student_feat, teacher_protos, student_protos):
    z = lax.axis_index("z")
    core = lax.axis_index("c")
    half = ROWS // NC
    together = lax.optimization_barrier

    def my_half(a):
        return lax.dynamic_slice_in_dim(a, core * half, half, 0)

    order = (z + jnp.array(OFFSETS, jnp.int32)) % NZ
    pos = jnp.concatenate([jnp.stack([z, core, lax.axis_index("x")]), order]).astype(jnp.int32)

    b0 = jnp.concatenate([my_half(teacher_feat), my_half(student_feat)], axis=1)
    u1, d1 = shift(b0, "z", 1), shift(b0, "z", -1)
    expo, cols = teacher(teacher_feat, teacher_protos)
    cols, u1, d1 = together((cols, u1, d1))

    u2, d2 = shift(u1, "z", 1), shift(d1, "z", -1)
    o0, ou1, od1 = swap_core(b0), swap_core(u1), swap_core(d1)
    got = gather(cols, ("x", "z"))
    s_dirs, tot, s_mix = student(student_feat, student_protos)
    got, u2, d2, o0, ou1, od1, tot = together((got, u2, d2, o0, ou1, od1, tot))

    u3, d3 = shift(u2, "z", 1), shift(d2, "z", -1)
    ou2, od2 = swap_core(u2), swap_core(d2)
    rows = row_pass(expo, got, tot)
    rows, u3, d3, ou2, od2 = together((rows, u3, d3, ou2, od2))
    u4 = shift(u3, "z", 1)
    got = gather(rows, ("y", "c"))
    got, u4 = together((got, u4))

    cols, tots = col_pass(expo, got, 1)
    cols = around(cols[0], "x").astype(bf16)
    cols = jnp.concatenate([cols, tots], axis=1)
    got2 = gather(jnp.broadcast_to(cols[None], (NZ,) + cols.shape), "z")

    got2, u3, d3, u4 = together((got2, u3, d3, u4))
    ou3, od3, ou4 = swap_core(u3), swap_core(d3), swap_core(u4)
    rows = row_pass(expo, got2, tot)
    rows, ou3, od3, ou4 = together((rows, ou3, od3, ou4))
    got = gather(rows, ("y", "c"))
    cols, _ = col_pass(expo, got, NX * NZ)

    got = gather(cols, ("x", "z"))
    rows_c, dirs_c, student_part = early(
        pos,
        [b0, u1, d1, u2, d2, u3, d3, u4],
        [o0, ou1, od1, ou2, od2, ou3, od3, ou4],
        teacher_protos.reshape(NX, NZ, DIM, DIM),
        s_dirs.reshape(NX, NZ, DIM, DIM),
        got2,
    )
    got, student_part = together((got, student_part))

    rows, col = row_last(expo, got)
    rows, col = together((rows, col))
    stat = gather(rows, ("z", "y", "c")).reshape(NZ, NY * NC, 4, 128)
    t_mix, cross = mix_pass(expo, col, s_dirs, student_feat)
    stat, t_mix, cross = together((stat, t_mix, cross))
    own, next1, next2, next3, keep, give, log_total = proto_part(
        pos, dirs_c, rows_c, stat, got2, student_part, col, s_mix, t_mix, cross
    )
    arrived = [shift(a, "x", d).astype(f32) for a, d in ((next1, 1), (next2, 2), (next3, 3))]
    proto_grad = ((own + arrived[0]) + (arrived[1] + arrived[2])).astype(bf16)

    terms, loss = unpacked(swap_core(give))
    mine = packed(keep[:half] + terms, keep[half : half + 1] + loss)
    terms, loss = unpacked(mine)
    away = [unpacked(shift(mine, "y", d)) for d in (1, 2, 3)]
    terms = (terms + away[1][0]) + (away[0][0] + away[2][0])
    loss = (loss + away[1][1]) + (away[0][1] + away[2][1])
    done = packed(terms, loss)
    there = swap_core(done)
    low, low_loss = unpacked(jnp.where(core == 0, done, there))
    high, high_loss = unpacked(jnp.where(core == 0, there, done))
    feature_grad = jnp.concatenate([low, high], axis=0).astype(bf16)
    row_loss = (log_total - jnp.concatenate([low_loss, high_loss], axis=1)).reshape(ROWS)
    return row_loss, feature_grad, proto_grad


def solution(mesh):
    fine = Mesh(mesh.devices.reshape(NX, NZ, NY, NC), ("x", "z", "y", "c"))
    rows, protos = P(("x", "z"), None), P(("y", "c"), None)
    return jax.shard_map(
        local,
        mesh=fine,
        in_specs=(rows, rows, protos, protos),
        out_specs=(P(("x", "z")), rows, P(("y", "c", "x", "z"), None)),
        check_vma=False,
    )
```

```python
import math

import jax
import jax.numpy as jnp
from jax import lax
from jax.experimental import pallas as pl
from jax.experimental.pallas import tpu as pltpu
from jax.sharding import Mesh, PartitionSpec as P

f32 = jnp.float32
bf16 = jnp.bfloat16

NX, NZ, NY, NC = 4, 8, 4, 2
DIM = 256
PROTOS = 65536
BATCH = 16384
ROWS = BATCH // (NX * NZ)
COLS = PROTOS // (NY * NC)
BK = 1024
NB = COLS // BK
T_EXP2 = math.log2(math.e) / 0.07
S_EXP2 = math.log2(math.e) / 0.1
FACTOR = PROTOS / (BATCH * 0.1)
VMEM = 60 * 1024 * 1024
SMALL = 24 * 1024 * 1024
MIDDLE = 48 * 1024 * 1024

NT = (((1,), (1,)), ((), ()))
NN = (((1,), (0,)), ((), ()))


def dot(a, b, dims):
    return lax.dot_general(a, b, dims, preferred_element_type=f32)


def unit_rows(x):
    xf = x.astype(f32)
    return (xf * lax.rsqrt(jnp.sum(xf * xf, axis=1, keepdims=True) + 1e-06)).astype(bf16)


def lane_fold(m):
    acc = m[:, :128]
    for i in range(1, m.shape[1] // 128):
        acc = acc + m[:, i * 128 : (i + 1) * 128]
    return acc


def to_lanes(acc):
    return jnp.sum(acc.T, axis=0, keepdims=True)


def rows4(v):
    return jnp.concatenate([v[:, i * 128 : (i + 1) * 128] for i in range(4)], axis=0)


def lanes512(m):
    return jnp.concatenate([m[i : i + 1] for i in range(4)], axis=1)


def call(kernel, ins, outs, out_shape, scratch, flops, nbytes, name, limit=VMEM):
    return pl.pallas_call(
        kernel,
        in_specs=ins,
        out_specs=outs,
        out_shape=out_shape,
        scratch_shapes=scratch,
        compiler_params=pltpu.CompilerParams(vmem_limit_bytes=limit),
        cost_estimate=pl.CostEstimate(flops=flops, bytes_accessed=nbytes, transcendentals=0),
        name=name,
    )


ANY = pl.BlockSpec(memory_space=pl.ANY)
OUTSIDE = pl.BlockSpec(memory_space=pltpu.HBM)
INSIDE = pl.BlockSpec(memory_space=pltpu.VMEM)
SCALARS = pl.BlockSpec(memory_space=pltpu.SMEM)
DMA = pltpu.SemaphoreType.DMA


def outside(a):
    return pltpu.with_memory_space_constraint(a, pltpu.HBM)


def begin(src, dst, sem):
    copy = pltpu.make_async_copy(src, dst, sem)
    copy.start()
    return copy


def begin_blocks(src, dst, sems):
    for j in range(NB):
        begin(src.at[j], dst.at[j], sems.at[j])


def shape(s, t):
    return jax.ShapeDtypeStruct(s, t)


def teacher_kernel(feat, protos, expo_o, cols_o, feat_s, protos_s, expo_s, logit_s, cols_s, sem, in_sems, out_sems):
    first = begin(feat, feat_s, sem)
    begin_blocks(protos, protos_s, in_sems)
    first.wait()
    feat_s[...] = unit_rows(feat_s[...])

    @pl.loop(0, NB)
    def _(j):
        pltpu.make_async_copy(protos.at[j], protos_s.at[j], in_sems.at[j]).wait()
        sums = []
        for n in range(BK // DIM):
            logit_s[n] = dot(feat_s[...], unit_rows(protos_s[j, n * DIM : (n + 1) * DIM, :]), NT)
            acc = jnp.zeros((8, DIM), f32)
            for r in range(0, ROWS, 64):
                e = jnp.exp2(logit_s[n, r : r + 64, :] * T_EXP2)
                expo_s[j, r : r + 64, n * DIM : (n + 1) * DIM] = e.astype(bf16)
                for q in range(0, 64, 8):
                    acc = acc + e[q : q + 8]
            sums.append(jnp.sum(acc, axis=0, keepdims=True))
        cols_s[pl.ds(j, 1), :] = jnp.concatenate(sums, axis=1)
        pltpu.make_async_copy(expo_s.at[j], expo_o.at[j], out_sems.at[j]).start()

    cols_o[...] = jnp.broadcast_to(cols_s[...].astype(bf16)[None], cols_o.shape)
    for j in range(NB):
        pltpu.make_async_copy(expo_s.at[j], expo_o.at[j], out_sems.at[j]).wait()


def teacher(feat, protos):
    return call(
        teacher_kernel,
        [ANY, ANY],
        [ANY, INSIDE],
        [shape((NB, ROWS, BK), bf16), shape((NX * NZ, NB, BK), bf16)],
        [
            pltpu.VMEM((ROWS, DIM), bf16),
            pltpu.VMEM((NB, BK, DIM), bf16),
            pltpu.VMEM((NB, ROWS, BK), bf16),
            pltpu.VMEM((BK // DIM, ROWS, DIM), f32),
            pltpu.VMEM((NB, BK), f32),
            DMA,
            DMA((NB,)),
            DMA((NB,)),
        ],
        2 * ROWS * COLS * DIM,
        ROWS * COLS * 2 + COLS * DIM * 2,
        "teacher",
    )(feat, protos.reshape(NB, BK, DIM))


def student_kernel(
    feat, protos, dirs_o, tot_o, mix_o, feat_s, protos_s, dirs_s, logit_s, exp_s, tot_s, sem, in_sems, out_sems
):
    first = begin(feat, feat_s, sem)
    begin_blocks(protos, protos_s, in_sems)
    first.wait()
    feat_s[...] = unit_rows(feat_s[...])
    tot_s[...] = jnp.zeros_like(tot_s)
    mix_o[...] = jnp.zeros_like(mix_o)

    @pl.loop(0, NB, unroll=2)
    def _(j):
        pltpu.make_async_copy(protos.at[j], protos_s.at[j], in_sems.at[j]).wait()
        for n in range(BK // DIM):
            part = slice(n * DIM, (n + 1) * DIM)
            dirs = unit_rows(protos_s[j, part, :])
            dirs_s[j, part, :] = dirs
            logit_s[n] = dot(feat_s[...], dirs, NT)
            for r in range(0, ROWS, 64):
                e = jnp.exp2(logit_s[n, r : r + 64, :] * S_EXP2)
                exp_s[r : r + 64, part] = e.astype(bf16)
                tot_s[r : r + 64, :] += lane_fold(e)
        mix_o[...] += dot(exp_s[...], dirs_s[j], NN)
        pltpu.make_async_copy(dirs_s.at[j], dirs_o.at[j], out_sems.at[j]).start()

    tot_o[...] = rows4(to_lanes(tot_s[...]))
    for j in range(NB):
        pltpu.make_async_copy(dirs_s.at[j], dirs_o.at[j], out_sems.at[j]).wait()


def student(feat, protos):
    return call(
        student_kernel,
        [ANY, ANY],
        [ANY, INSIDE, INSIDE],
        [shape((NB, BK, DIM), bf16), shape((4, 128), f32), shape((ROWS, DIM), f32)],
        [
            pltpu.VMEM((ROWS, DIM), bf16),
            pltpu.VMEM((NB, BK, DIM), bf16),
            pltpu.VMEM((NB, BK, DIM), bf16),
            pltpu.VMEM((BK // DIM, ROWS, DIM), f32),
            pltpu.VMEM((ROWS, BK), bf16),
            pltpu.VMEM((ROWS, 128), f32),
            DMA,
            DMA((NB,)),
            DMA((NB,)),
        ],
        4 * ROWS * COLS * DIM,
        COLS * DIM * 4,
        "student",
    )(feat, protos.reshape(NB, BK, DIM))


def col_scale(got):
    return 1.0 / (PROTOS * jnp.sum(got[...].astype(f32), axis=0))


def scaled_rows(expo, col, acc_s, j):
    c = col[pl.ds(j, 1), :]
    cs = [c[:, g * 128 : (g + 1) * 128] for g in range(BK // 128)]
    for r in range(0, ROWS, 32):
        acc = acc_s[r : r + 32, :]
        for g in range(BK // 128):
            acc = acc + expo[j, r : r + 32, g * 128 : (g + 1) * 128].astype(f32) * cs[g]
        acc_s[r : r + 32, :] = acc


def row_sums(expo, got, col, acc_s):
    acc_s[...] = jnp.zeros_like(acc_s)
    col[...] = col_scale(got[:, :, :BK])

    @pl.loop(0, NB)
    def _(j):
        scaled_rows(expo, col, acc_s, j)

    return rows4(to_lanes(acc_s[...]))


def row_kernel(expo, got, tot, rows_o, col_s, acc_s, tot_s, sem):
    first = begin(tot, tot_s, sem)
    part = row_sums(expo, got, col_s, acc_s)
    first.wait()
    part = jnp.concatenate([part, tot_s[...]], axis=0)
    rows_o[...] = jnp.broadcast_to(part[None], rows_o.shape)


def row_pass(held, got, tot):
    return call(
        row_kernel,
        [INSIDE, INSIDE, OUTSIDE],
        INSIDE,
        shape((NY * NC, 8, 128), f32),
        [pltpu.VMEM((NB, BK), f32), pltpu.VMEM((ROWS, 128), f32), pltpu.VMEM((4, 128), f32), DMA],
        2 * ROWS * COLS,
        1 << 16,
        "row_pass",
        SMALL,
    )(pltpu.with_memory_space_constraint(held, pltpu.VMEM), got, outside(tot))


def row_last_kernel(expo, got, rows_o, col_o, acc_s):
    part = row_sums(expo, got, col_o, acc_s)
    rows_o[...] = jnp.broadcast_to(part[None], rows_o.shape)


def row_last(held, got):
    return call(
        row_last_kernel,
        [INSIDE, INSIDE],
        [INSIDE, INSIDE],
        [shape((NZ * NY * NC, 4, 128), f32), shape((NB, BK), f32)],
        [pltpu.VMEM((ROWS, 128), f32)],
        2 * ROWS * COLS,
        1 << 16,
        "row_last",
        SMALL,
    )(pltpu.with_memory_space_constraint(held, pltpu.VMEM), got)


def col_kernel(expo, got, cols_o, tot_o, scale_s, cols_s):
    total = jnp.sum(got[...], axis=0)
    scale_s[...] = jnp.broadcast_to(1.0 / (BATCH * lanes512(total[:4])), (128, ROWS)).T

    @pl.loop(0, NB)
    def _(j):
        accs = [jnp.zeros((8, 128), f32)] * (BK // 128)
        for r in range(0, ROWS, 32):
            scale = scale_s[r : r + 32, :]
            for g in range(BK // 128):
                t = expo[j, r : r + 32, g * 128 : (g + 1) * 128].astype(f32) * scale
                accs[g] = accs[g] + ((t[0:8] + t[8:16]) + (t[16:24] + t[24:32]))
        cols_s[pl.ds(j, 1), :] = jnp.concatenate(
            [jnp.sum(a, axis=0, keepdims=True) for a in accs], axis=1
        )

    cols_o[...] = jnp.broadcast_to(cols_s[...].astype(bf16)[None], cols_o.shape)
    hi = total[4:].astype(bf16).astype(f32)
    tot_o[...] = jnp.concatenate([hi, total[4:] - hi], axis=0).astype(bf16)


def col_pass(held, got, copies):
    return call(
        col_kernel,
        [INSIDE, INSIDE],
        [INSIDE, INSIDE],
        [shape((copies, NB, BK), bf16), shape((8, 128), bf16)],
        [pltpu.VMEM((ROWS, 128), f32), pltpu.VMEM((NB, BK), f32)],
        2 * ROWS * COLS,
        1 << 20,
        "col_pass",
        SMALL,
    )(pltpu.with_memory_space_constraint(held, pltpu.VMEM), got)


def mix_kernel(expo, col, dirs, feat, mix_o, cross_o, expo_s, dirs_s, feat_s, w_s, sem, sems):
    for j in range(NB):
        begin(expo.at[j], expo_s.at[j], sems.at[0, j])
        begin(dirs.at[j], dirs_s.at[j], sems.at[1, j])
    first = begin(feat, feat_s, sem)
    mix_o[...] = jnp.zeros_like(mix_o)

    @pl.loop(0, NB)
    def _(j):
        pltpu.make_async_copy(expo.at[j], expo_s.at[j], sems.at[0, j]).wait()
        c = col[pl.ds(j, 1), :]
        cs = [c[:, g * 128 : (g + 1) * 128] for g in range(BK // 128)]
        for r in range(0, ROWS, 32):
            for g in range(BK // 128):
                part = slice(g * 128, (g + 1) * 128)
                w_s[r : r + 32, part] = (expo_s[j, r : r + 32, part].astype(f32) * cs[g]).astype(bf16)
        pltpu.make_async_copy(dirs.at[j], dirs_s.at[j], sems.at[1, j]).wait()
        mix_o[...] += dot(w_s[...], dirs_s[j], NN)

    first.wait()
    unit = unit_rows(feat_s[...]).astype(f32)
    cross_o[...] = to_lanes(lane_fold(mix_o[...] * unit)) / 0.1


def mix_pass(expo, col, dirs, feat):
    return call(
        mix_kernel,
        [ANY, INSIDE, ANY, ANY],
        [INSIDE, INSIDE],
        [shape((ROWS, DIM), f32), shape((1, ROWS), f32)],
        [
            pltpu.VMEM((NB, ROWS, BK), bf16),
            pltpu.VMEM((NB, BK, DIM), bf16),
            pltpu.VMEM((ROWS, DIM), bf16),
            pltpu.VMEM((ROWS, BK), bf16),
            DMA,
            DMA((2, NB)),
        ],
        2 * ROWS * COLS * DIM,
        ROWS * COLS * 2 + COLS * DIM * 2,
        "mix_pass",
    )(expo, pltpu.with_memory_space_constraint(col, pltpu.VMEM), dirs, feat)


def early_kernel(*refs):
    pos, mine, other = refs[0], refs[1 : 1 + NZ], refs[1 + NZ : 1 + 2 * NZ]
    (t_protos, s_dirs, got, rows_o, dirs_o, grad_o,
     raw_s, rows_s, t_s, s_s, got_s, d_s, small, sems, outs) = refs[1 + 2 * NZ :]
    z, core = pos[0], pos[1]
    for k in range(NZ):
        begin(mine[k], raw_s.at[k, core], sems.at[0, k])
        begin(other[k], raw_s.at[k, 1 - core], sems.at[1, k])
        if k == 0:
            first = [begin(t_protos.at[i, z], t_s.at[pl.ds(i * DIM, DIM)], small.at[i]) for i in range(NX)]
            first += [begin(s_dirs.at[i, z], s_s.at[pl.ds(i * DIM, DIM)], small.at[NX + i]) for i in range(NX)]
            first.append(begin(got, got_s, small.at[2 * NX]))
    grad_o[...] = jnp.zeros_like(grad_o)
    for copy in first:
        copy.wait()
    dirs_o[...] = unit_rows(t_s[...])

    @pl.loop(0, NZ, unroll=2)
    def _(k):
        pltpu.make_async_copy(mine[0], raw_s.at[k, core], sems.at[0, k]).wait()
        pltpu.make_async_copy(other[0], raw_s.at[k, 1 - core], sems.at[1, k]).wait()
        total = got_s[pos[3 + k]].astype(f32)[:, BK:]
        scale = FACTOR / lanes512(total[:4] + total[4:])
        half = ROWS // NC
        for h in range(NC):
            part = slice(h * half, (h + 1) * half)
            rows_s[k, part, :DIM] = unit_rows(raw_s[k, h, :, :DIM])
            rows_s[k, part, DIM:] = unit_rows(raw_s[k, h, :, DIM:])
        pltpu.make_async_copy(rows_s.at[k], rows_o.at[k], outs.at[k]).start()
        s_rows = rows_s[k, :, DIM:]
        d_s[...] = (jnp.exp2(dot(s_s[...], s_rows, NT) * S_EXP2) * scale).astype(bf16)
        grad_o[...] += dot(d_s[...], s_rows, NN)

    for k in range(NZ):
        pltpu.make_async_copy(rows_s.at[k], rows_o.at[k], outs.at[k]).wait()


def early(pos, mine, other, t_protos, s_dirs, got):
    n, half = NX * DIM, ROWS // NC
    return call(
        early_kernel,
        [SCALARS] + [ANY] * (2 * NZ + 3),
        [ANY, INSIDE, INSIDE],
        [shape((NZ, ROWS, 2 * DIM), bf16), shape((n, DIM), bf16), shape((n, DIM), f32)],
        [
            pltpu.VMEM((NZ, NC, half, 2 * DIM), bf16),
            pltpu.VMEM((NZ, ROWS, 2 * DIM), bf16),
            pltpu.VMEM((n, DIM), bf16),
            pltpu.VMEM((n, DIM), bf16),
            pltpu.VMEM(got.shape, bf16),
            pltpu.VMEM((n, ROWS), bf16),
            DMA((2 * NX + 1,)),
            DMA((2, NZ)),
            DMA((NZ,)),
        ],
        4 * ROWS * COLS * DIM,
        ROWS * COLS,
        "early",
    )(pos, *mine, *other, t_protos, s_dirs, got)


def down_rows(v):
    return jnp.broadcast_to(v, (128, v.shape[1])).T


def scale_rows(m, scale):
    return jnp.concatenate([m[:, g : g + 128] * scale for g in range(0, m.shape[1], 128)], axis=1)


def grad_kernel(
    pos, dirs, rows, stat, got, student_part, col, s_mix, t_mix, cross,
    own_o, next1_o, next2_o, next3_o, keep_o, give_o, line_o,
    rows_s, got_s, dirs_s, part_s, acc_s, s_mix_s, t_mix_s, cross_s, small, sems,
):
    z, core, x = pos[0], pos[1], pos[2]
    first = [begin(dirs, dirs_s, small.at[1])]
    for k in range(NZ):
        begin(rows.at[k], rows_s.at[k], sems.at[k])
    second = [
        begin(got.at[pl.ds(z, 1)], got_s, small.at[2]),
        begin(s_mix, s_mix_s, small.at[3]),
        begin(t_mix, t_mix_s, small.at[4]),
        begin(cross, cross_s, small.at[0]),
        begin(student_part, part_s, small.at[5]),
    ]
    acc_s[...] = jnp.zeros_like(acc_s)
    for copy in first:
        copy.wait()

    @pl.loop(0, NZ, unroll=2)
    def _(k):
        total = jnp.sum(stat[pos[3 + k]], axis=0)
        scale = down_rows(FACTOR / lanes512(total))
        pltpu.make_async_copy(rows.at[k], rows_s.at[k], sems.at[k]).wait()
        expo = jnp.exp2(dot(dirs_s[...], rows_s[k, :, :DIM], NT) * T_EXP2).astype(bf16)
        r = scale_rows(rows_s[k, :, DIM:].astype(f32), scale).astype(bf16)
        acc_s[...] += dot(expo, r, NN)

    for copy in second:
        copy.wait()
    for d in range(NX):
        i = lax.rem(x + d, NX)
        c = col[pl.ds(2 * i + z // 4, 1), :]
        c = sum(jnp.where(lax.rem(z, 4) == q, c[:, q * DIM : (q + 1) * DIM], 0.0) for q in range(4))
        part = pl.ds(pl.multiple_of(i * DIM, DIM), DIM)
        block = part_s[part, :] - scale_rows(acc_s[part, :], down_rows(c))
        if d == 0:
            own_o[...] = block
        else:
            (next1_o, next2_o, next3_o)[d - 1][...] = block.astype(bf16)

    row_total = lanes512(jnp.sum(stat[z], axis=0))
    total = got_s[0].astype(f32)[:, BK:]
    total = lanes512(total[:4] + total[4:])
    s_mix_s[...] = scale_rows(s_mix_s[...], down_rows(FACTOR / total)) - scale_rows(
        t_mix_s[...], down_rows(FACTOR / row_total)
    )
    half = ROWS // NC
    keep_o[:half, :] = s_mix_s[pl.ds(pl.multiple_of(core * half, half), half), :]
    give_o[:half, :] = s_mix_s[pl.ds(pl.multiple_of((1 - core) * half, half), half), :].astype(bf16)
    loss = cross_s[...] / row_total
    low, high = loss[:, :half], loss[:, half:]
    away = jnp.where(core == 0, high, low)
    hi = away.astype(bf16).astype(f32)
    zeros = jnp.zeros((14, DIM), f32)
    give_o[half:, :] = jnp.concatenate([hi, away - hi, zeros], axis=0).astype(bf16)
    keep_o[half:, :] = jnp.concatenate([jnp.where(core == 0, low, high), zeros[:7]], axis=0)
    line_o[...] = jnp.log(total)


def proto_part(pos, dirs, rows, stat, got, student_part, col, s_mix, t_mix, cross):
    n, half = NX * DIM, ROWS // NC
    return call(
        grad_kernel,
        [SCALARS, ANY, ANY, INSIDE, ANY, ANY, INSIDE, ANY, OUTSIDE, OUTSIDE],
        [INSIDE] * 7,
        [
            shape((DIM, DIM), f32),
            shape((DIM, DIM), bf16),
            shape((DIM, DIM), bf16),
            shape((DIM, DIM), bf16),
            shape((half + 8, DIM), f32),
            shape((half + 16, DIM), bf16),
            shape((1, ROWS), f32),
        ],
        [
            pltpu.VMEM((NZ, ROWS, 2 * DIM), bf16),
            pltpu.VMEM((1,) + got.shape[1:], bf16),
            pltpu.VMEM((n, DIM), bf16),
            pltpu.VMEM((n, DIM), f32),
            pltpu.VMEM((n, DIM), f32),
            pltpu.VMEM((ROWS, DIM), f32),
            pltpu.VMEM((ROWS, DIM), f32),
            pltpu.VMEM((1, ROWS), f32),
            DMA((6,)),
            DMA((NZ,)),
        ],
        4 * ROWS * COLS * DIM,
        ROWS * COLS,
        "proto_part",
        MIDDLE,
    )(pos, dirs, rows, stat, got, student_part, col, s_mix, outside(t_mix), outside(cross))


def gather(a, axes):
    return lax.all_to_all(a, axes, 0, 0)


def swap_core(a):
    return lax.ppermute(a, "c", [(0, 1), (1, 0)])


def shift(a, axis, by):
    n = lax.axis_size(axis)
    return lax.ppermute(a, axis, [(i, (i + by) % n) for i in range(n)])


OFFSETS = (0, -1, 1, -2, 2, -3, 3, -4)


def packed(terms, loss):
    hi = lax.reduce_precision(loss, 8, 7)
    tail = jnp.concatenate([hi, loss - hi, jnp.zeros((14, DIM), f32)], axis=0)
    return jnp.concatenate([terms, tail], axis=0).astype(bf16)


def unpacked(a):
    a = a.astype(f32)
    n = a.shape[0] - 16
    return a[:n], a[n : n + 1] + a[n + 1 : n + 2]


def around(a, axis):
    one, two, three = [shift(a, axis, d).astype(f32) for d in (1, 2, 3)]
    return (a.astype(f32) + two) + (one + three)


def local(teacher_feat, student_feat, teacher_protos, student_protos):
    z = lax.axis_index("z")
    core = lax.axis_index("c")
    half = ROWS // NC
    together = lax.optimization_barrier

    def my_half(a):
        return lax.dynamic_slice_in_dim(a, core * half, half, 0)

    order = (z + jnp.array(OFFSETS, jnp.int32)) % NZ
    pos = jnp.concatenate([jnp.stack([z, core, lax.axis_index("x")]), order]).astype(jnp.int32)

    b0 = jnp.concatenate([my_half(teacher_feat), my_half(student_feat)], axis=1)
    u1, d1 = shift(b0, "z", 1), shift(b0, "z", -1)
    expo, cols = teacher(teacher_feat, teacher_protos)
    cols, u1, d1 = together((cols, u1, d1))

    u2, d2 = shift(u1, "z", 1), shift(d1, "z", -1)
    o0, ou1, od1 = swap_core(b0), swap_core(u1), swap_core(d1)
    got = gather(cols, ("x", "z"))
    s_dirs, tot, s_mix = student(student_feat, student_protos)
    got, u2, d2, o0, ou1, od1, tot = together((got, u2, d2, o0, ou1, od1, tot))

    u3, d3 = shift(u2, "z", 1), shift(d2, "z", -1)
    ou2, od2 = swap_core(u2), swap_core(d2)
    rows = row_pass(expo, got, tot)
    rows, u3, d3, ou2, od2 = together((rows, u3, d3, ou2, od2))
    u4 = shift(u3, "z", 1)
    got = gather(rows, ("y", "c"))
    got, u4 = together((got, u4))

    cols, tots = col_pass(expo, got, 1)
    cols = around(cols[0], "x").astype(bf16)
    cols = jnp.concatenate([cols, tots], axis=1)
    got2 = gather(jnp.broadcast_to(cols[None], (NZ,) + cols.shape), "z")

    got2, u3, d3, u4 = together((got2, u3, d3, u4))
    ou3, od3, ou4 = swap_core(u3), swap_core(d3), swap_core(u4)
    rows = row_pass(expo, got2, tot)
    rows, ou3, od3, ou4 = together((rows, ou3, od3, ou4))
    got = gather(rows, ("y", "c"))
    cols, _ = col_pass(expo, got, NX * NZ)

    got = gather(cols, ("x", "z"))
    rows_c, dirs_c, student_part = early(
        pos,
        [b0, u1, d1, u2, d2, u3, d3, u4],
        [o0, ou1, od1, ou2, od2, ou3, od3, ou4],
        teacher_protos.reshape(NX, NZ, DIM, DIM),
        s_dirs.reshape(NX, NZ, DIM, DIM),
        got2,
    )
    got, student_part = together((got, student_part))

    rows, col = row_last(expo, got)
    rows, col = together((rows, col))
    stat = gather(rows, ("z", "y", "c")).reshape(NZ, NY * NC, 4, 128)
    t_mix, cross = mix_pass(expo, col, s_dirs, student_feat)
    stat, t_mix, cross = together((stat, t_mix, cross))
    own, next1, next2, next3, keep, give, log_total = proto_part(
        pos, dirs_c, rows_c, stat, got2, student_part, col, s_mix, t_mix, cross
    )
    arrived = [shift(a, "x", d).astype(f32) for a, d in ((next1, 1), (next2, 2), (next3, 3))]
    proto_grad = ((own + arrived[0]) + (arrived[1] + arrived[2])).astype(bf16)

    terms, loss = unpacked(swap_core(give))
    mine = packed(keep[:half] + terms, keep[half : half + 1] + loss)
    terms, loss = unpacked(mine)
    away = [unpacked(shift(mine, "y", d)) for d in (1, 2, 3)]
    terms = (terms + away[1][0]) + (away[0][0] + away[2][0])
    loss = (loss + away[1][1]) + (away[0][1] + away[2][1])
    done = packed(terms, loss)
    there = swap_core(done)
    low, low_loss = unpacked(jnp.where(core == 0, done, there))
    high, high_loss = unpacked(jnp.where(core == 0, there, done))
    feature_grad = jnp.concatenate([low, high], axis=0).astype(bf16)
    row_loss = (log_total - jnp.concatenate([low_loss, high_loss], axis=1)).reshape(ROWS)
    return row_loss, feature_grad, proto_grad


def solution(mesh):
    fine = Mesh(mesh.devices.reshape(NX, NZ, NY, NC), ("x", "z", "y", "c"))
    rows, protos = P(("x", "z"), None), P(("y", "c"), None)
    return jax.shard_map(
        local,
        mesh=fine,
        in_specs=(rows, rows, protos, protos),
        out_specs=(P(("x", "z")), rows, P(("y", "c", "x", "z"), None)),
        check_vma=False,
    )
```
